256 devices in a mesh: row: 16 (over y, x_lo, core), col: 16 (over x_hi, z).
Axes of the slice: x: 4 (x_hi: 2, x_lo: 2; x = x_hi * 2 + x_lo), y: 4, z: 8, core: 2. Of those that a mesh axis runs over, the one named last changes fastest.
Arguments:
- tokens: bfloat16 [1536, 8192], P('col', 'row'), may hold values from -6 to 6
- gate_weight: bfloat16 [8192, 29568], P('row', 'col'), may hold values from -0.0625 to 0.0625
- up_weight: bfloat16 [8192, 29568], P('row', 'col'), may hold values from -0.0625 to 0.0625
- gate_lower: bfloat16 [16, 8192, 64], P('col', 'row'), may hold values from -0.0625 to 0.0625
- up_lower: bfloat16 [16, 8192, 64], P('col', 'row'), may hold values from -0.0625 to 0.0625
- gate_upper: bfloat16 [16, 64, 29568], P('row', None, 'col'), may hold values from -0.21875 to 0.21875
- up_upper: bfloat16 [16, 64, 29568], P('row', None, 'col'), may hold values from -0.21875 to 0.21875
- outgoing: int32 [1], replicated, may hold values from 0 to 15
- incoming: int32 [1], replicated, may hold values from 0 to 15
Outputs:
- new_gate: bfloat16 [8192, 29568], P('row', 'col')
- new_up: bfloat16 [8192, 29568], P('row', 'col')
- hidden: bfloat16 [1536, 29568], P('row', 'col')
The draws below stay inside these ranges and needn't reach their ends.
All inputs are finite; a program needn't handle non-finite values.
Results may differ from the reference program's by a relative error of at most 0.0058.
Values may be sent and summed in bfloat16 or wider, within the bound.
A program may use at most 128 MiB of HBM per device.

```python
import jax
import jax.numpy as jnp
from jax import lax

D = 8192
FF = 29568
R = 64
TENANTS = 16
TOKENS = 1536
N_ROW = 16


def levels(rng, dims, cuts, smallest, largest):
    level = 1.0
    for dim, blocks in cuts:
        draws = jax.random.uniform(jax.random.fold_in(jax.random.fold_in(rng, 6), dim), (blocks,), jnp.float32, smallest / len(cuts), largest / len(cuts))
        level = level * jnp.repeat(jnp.exp(draws), dims[dim] // blocks).reshape((-1,) + (1,) * (len(dims) - 1 - dim))
    return level


def normal_values(own_key, extent, deviation, limit, pieces=(), held_as=jnp.bfloat16):
    values = deviation * jax.random.normal(own_key, extent, jnp.float32)
    if pieces:
        values = values * levels(own_key, extent, pieces, -0.22, 0.18)
    return jnp.clip(values, -limit, limit).astype(held_as)


def setup_inputs(seed: int = 0) -> dict:
    arg_keys = jax.random.split(jax.random.key(seed), 10)
    tokens = normal_values(arg_keys[0], (TOKENS, D), 1.0, 6.0, ((0, 16), (1, 16)))
    gate_weight = normal_values(arg_keys[1], (D, FF), D ** -0.5, 0.0625, ((0, 16), (1, 16)))
    up_weight = normal_values(arg_keys[2], (D, FF), D ** -0.5, 0.0625, ((0, 16), (1, 16)))
    gate_lower = normal_values(arg_keys[3], (TENANTS, D, R), D ** -0.5, 0.0625, ((0, 16), (1, 16)))
    up_lower = normal_values(arg_keys[4], (TENANTS, D, R), D ** -0.5, 0.0625, ((0, 16), (1, 16)))
    gate_upper = normal_values(arg_keys[5], (TENANTS, R, FF), (12 * R) ** -0.5, 0.21875, ((0, 16), (2, 16)))
    up_upper = normal_values(arg_keys[6], (TENANTS, R, FF), (12 * R) ** -0.5, 0.21875, ((0, 16), (2, 16)))
    outgoing = jax.random.randint(arg_keys[7], (1,), 0, TENANTS).astype(jnp.int32)
    incoming = jax.random.randint(arg_keys[8], (1,), 0, TENANTS).astype(jnp.int32)
    return dict(tokens=tokens, gate_weight=gate_weight, up_weight=up_weight, gate_lower=gate_lower, up_lower=up_lower, gate_upper=gate_upper, up_upper=up_upper, outgoing=outgoing, incoming=incoming)


def merge_one(weight, lower, upper, old, new):
    lower_old = lax.dynamic_index_in_dim(lower, old, 0, keepdims=False)
    lower_new = lax.dynamic_index_in_dim(lower, new, 0, keepdims=False)
    upper_old = lax.dynamic_index_in_dim(upper, old, 0, keepdims=False)
    upper_new = lax.dynamic_index_in_dim(upper, new, 0, keepdims=False)
    blocks = N_ROW
    weight_blocks = weight.reshape(blocks, D // blocks, FF)
    lower_old = lower_old.reshape(blocks, D // blocks, R)
    lower_new = lower_new.reshape(blocks, D // blocks, R)

    def one_block(items):
        w_block, l_old, l_new = items
        delta = jnp.dot(l_new, upper_new, preferred_element_type=jnp.float32) - jnp.dot(l_old, upper_old, preferred_element_type=jnp.float32)
        return (w_block.astype(jnp.float32) + delta).astype(jnp.bfloat16)

    merged = lax.map(one_block, (weight_blocks, lower_old, lower_new))
    return merged.reshape(D, FF)


def reference(tokens, gate_weight, up_weight, gate_lower, up_lower, gate_upper, up_upper, outgoing, incoming):
    old = outgoing[0].astype(jnp.int32)
    new = incoming[0].astype(jnp.int32)
    new_gate = merge_one(gate_weight, gate_lower, gate_upper, old, new)
    new_up = merge_one(up_weight, up_lower, up_upper, old, new)
    gate = jnp.dot(tokens, new_gate, preferred_element_type=jnp.float32)
    up = jnp.dot(tokens, new_up, preferred_element_type=jnp.float32)
    hidden = (jax.nn.silu(gate) * up).astype(jnp.bfloat16)
    return new_gate, new_up, hidden
```

```python
import jax
import jax.numpy as jnp
from jax import lax
from jax.experimental import pallas as pl
from jax.experimental.pallas import tpu as pltpu
from jax.sharding import PartitionSpec as P

MESH = pl.DeviceIdType.MESH
BF, F32 = jnp.bfloat16, jnp.float32
ROWS, DEPTH, FF, RANK = 96, 512, 1848, 64
WIDE, CHUNKS = 256, 7
MAIN = WIDE * CHUNKS
LAST = FF - MAIN
CROSS = (0, 2, 4)
ALONG = (1, 3, 5, 6)


class Semaphores:
    def __init__(self):
        self.names = {}

    def of(self, *name):
        return self.names.setdefault(name, len(self.names))


def kernel(
    tok, gw, uw, gl, ul, gu, uu, out_s, inc_s,
    ng, nu, hid,
    T, wg, wu, vg, vu, wc, wt, pad, lc, lr, lf, uc, u0, us, ur, uf,
    part, parts_last, rx, qo, qa, ro, ra, acc, fs, fx, to, ta, tacc, ts, tx,
    ssem, rsem, lsem,
):
    row, col = lax.axis_index("row"), lax.axis_index("col")
    k, chip = row % 2, row // 2
    y, xm = row // 4, (row // 2) % 2
    xo = 1 - xm
    yp, yo, ym = (y + 1) % 4, (y + 2) % 4, (y + 3) % 4
    xh, z = col // 8, col % 8
    names = Semaphores()

    partner = (chip * 2 + 1 - k, col)
    cross = (y * 4 + xo * 2 + k, col)
    up_y = (yp * 4 + xm * 2 + k, col)
    down_y = (ym * 4 + xm * 2 + k, col)
    far_x = (row, (1 - xh) * 8 + z)
    up_z = (row, xh * 8 + (z + 1) % 8)
    down_z = (row, xh * 8 + (z + 7) % 8)

    def copy(src, dst, target, index):
        return pltpu.make_async_remote_copy(
            src_ref=src, dst_ref=dst, send_sem=ssem.at[index], recv_sem=rsem.at[index],
            device_id=target, device_id_type=MESH,
        )

    sent = []

    def send(src, dst, target, *name):
        c = copy(src, dst, target, names.of(*name))
        c.start()
        sent.append(c)
        return c

    load_g = pltpu.make_async_copy(gw, wg, lsem.at[0])
    load_u = pltpu.make_async_copy(uw, wu, lsem.at[1])
    load_g.start()
    load_u.start()

    new, old = inc_s[0], out_s[0]
    zero = jnp.zeros((), BF)
    for m, ref in enumerate((gu, uu)):
        b = ref[0]
        uc[m, 0:4] = jnp.where(new == row, b, jnp.zeros_like(b)).reshape(4, 16, FF)
        uc[m, 4:8] = jnp.where(old == row, -b, jnp.zeros_like(b)).reshape(4, 16, FF)
    for m, ref in enumerate((gl, ul)):
        a = ref[0]
        both = jnp.concatenate(
            [jnp.where(new == col, a, jnp.zeros_like(a)), jnp.where(old == col, a, jnp.zeros_like(a))], axis=1
        )
        lc[:, m] = both.reshape(16, 32, 128)

    barrier = pltpu.get_barrier_semaphore()
    pl.semaphore_signal(barrier, inc=1, device_id=partner, device_id_type=MESH)
    for i in range(1, 8):
        pl.semaphore_signal(barrier, inc=1, device_id=((chip + i) % 8 * 2 + k, col), device_id_type=MESH)
    for i in range(1, 16):
        pl.semaphore_signal(barrier, inc=1, device_id=(row, (col + i) % 16), device_id_type=MESH)
    pl.semaphore_wait(barrier, 23)

    even = k == z % 2
    xs, ys = (z // 2) % 2, col // 4
    t0 = copy(tok, T.at[xs, ys, :, DEPTH:], partner, names.of("t0"))

    @pl.when(jnp.logical_not(even))
    def _():
        t0.start()

    @pl.when(even)
    def _():
        T[xs, ys, :, 0:DEPTH] = tok[...]

    c_u0 = send(uc.at[1 - k], u0, partner, "u0")
    l1 = [send(lc.at[(col + i) % 16], lr.at[i - 1], (row, (col + i) % 16), "l1", i) for i in range(1, 16)]

    def block(zz, q):
        return T.at[(zz // 2) % 2, (xh + q) % 2 * 2 + zz // 4]

    def hop(direction, stage, q, zz):
        target = (up_z, down_z)[direction]
        return copy(block(zz, q), block(zz, q), target, names.of("z", direction, stage, q))

    def source(direction, distance):
        return (z - distance + 8) % 8 if direction == 0 else (z + distance) % 8

    far = copy(block(z, 0), block(z, 0), far_x, names.of("h"))
    far_in = copy(block(z, 1), block(z, 1), far_x, names.of("h"))

    @pl.when(even)
    def _():
        t0.wait_recv()
        far.start()
        for d in range(2):
            hop(d, 1, 0, z).start()

    c_u0.wait_recv()
    us[...] = uc[k] + u0[...]
    u1 = [send(us.at[(chip + i) % 8], ur.at[i - 1], ((chip + i) % 8 * 2 + k, col), "u1", i) for i in range(1, 8)]

    @pl.when(even)
    def _():
        far_in.wait_recv()
        for d in range(2):
            hop(d, 1, 1, z).start()

    @pl.when(jnp.logical_not(even))
    def _():
        for q in range(2):
            for d in range(2):
                hop(d, 1, q, source(d, 1)).wait_recv()
                hop(d, 2, q, source(d, 1)).start()

    for c in u1:
        c.wait_recv()
    total = us[chip].astype(F32)
    for i in range(7):
        total = total + ur[i].astype(F32)
    uf[k, chip] = total.astype(BF)
    u2 = [send(uf.at[k, chip], uf.at[k, chip], ((chip + i) % 8 * 2 + k, col), "u2", i) for i in range(1, 8)]
    u3 = [send(uf.at[k, chip], uf.at[k, chip], partner, "u3", 0)]

    for c in l1:
        c.wait_recv()
    total = lc[col].astype(F32)
    for i in range(15):
        total = total + lr[i].astype(F32)
    lf[col] = total.astype(BF)
    l2 = [send(lf.at[col], lf.at[col], (row, (col + i) % 16), "l2", i) for i in range(1, 16)]

    @pl.when(even)
    def _():
        for q in range(2):
            for d in range(2):
                hop(d, 2, q, source(d, 2)).wait_recv()
                hop(d, 3, q, source(d, 2)).start()

    for i in range(1, 8):
        u2[i - 1].wait_recv()
        s = (chip - i + 8) % 8
        u3.append(send(uf.at[k, s], uf.at[k, s], partner, "u3", i))

    @pl.when(jnp.logical_not(even))
    def _():
        for q in range(2):
            for d in range(2):
                hop(d, 3, q, source(d, 3)).wait_recv()
                if d == q:
                    hop(d, 4, q, source(d, 3)).start()

    for c in l2:
        c.wait_recv()
    for c in u3:
        c.wait_recv()
    load_g.wait()
    load_u.wait()

    def swap(j):
        return copy(wc.at[j, :, 0:DEPTH], wc.at[j, :, DEPTH:], partner, first_swap + j)

    for j in range(CHUNKS):
        index = names.of("w", j)
        if j == 0:
            first_swap = index

    def merge(j, carry):
        cols = pl.ds(pl.multiple_of(j * WIDE, WIDE), WIDE)
        for m, (w, v) in enumerate(((wg, vg), (wu, vu))):
            delta = jnp.dot(
                lf[:, m].reshape(DEPTH, 2 * RANK), uf[m, :, :, cols].reshape(2 * RANK, WIDE),
                preferred_element_type=F32,
            )
            merged = (w[:, cols].astype(F32) + delta).astype(BF)
            v[:, cols] = merged
            wc[j, m, 0:DEPTH] = merged
        swap(j).start()
        return carry

    lax.fori_loop(0, CHUNKS, merge, 0)
    pad[...] = jnp.zeros_like(pad)
    for m, (w, v) in enumerate(((wg, vg), (wu, vu))):
        delta = jnp.dot(
            lf[:, m].reshape(DEPTH, 2 * RANK), uf[m, :, :, MAIN:FF].reshape(2 * RANK, LAST),
            preferred_element_type=F32,
        )
        merged = (w[:, MAIN:FF].astype(F32) + delta).astype(BF)
        v[:, MAIN:FF] = merged
        pad[m, :, 0:LAST] = merged.astype(F32)
    wt[0:DEPTH] = (pad[0] + pltpu.roll(pad[1], 64, 1)).astype(BF)
    c_wt = send(wt.at[0:DEPTH], wt.at[DEPTH:], partner, "wt")
    store_g = pltpu.make_async_copy(vg, ng, lsem.at[2])
    store_u = pltpu.make_async_copy(vu, nu, lsem.at[3])
    store_g.start()
    store_u.start()

    @pl.when(even)
    def _():
        hop(0, 4, 0, source(0, 4)).wait_recv()
        hop(1, 4, 1, source(1, 4)).wait_recv()

    def compute(j):
        swap(j).wait_recv()

        def quarter(i, carry):
            m, x = i // 2, i % 2
            p = jnp.dot(T[x].reshape(4 * ROWS, 2 * DEPTH), wc[j, m], preferred_element_type=F32)
            part[j, m, x] = p.astype(BF).reshape(4, ROWS, WIDE)
            return carry

        lax.fori_loop(0, 4, quarter, 0)

    def compute_last():
        c_wt.wait_recv()
        for x in range(2):
            p = jnp.dot(T[x].reshape(4 * ROWS, 2 * DEPTH), wt[...], preferred_element_type=F32)
            parts_last[x] = p.astype(BF).reshape(4, ROWS, 128)

    def add(ref, other):
        ref[...] = (ref[...].astype(F32) + other[...].astype(F32)).astype(BF)

    def finish(j, gate, up):
        h = gate / (1 + jnp.exp(-gate)) * up
        hid[:, j * WIDE:(j + 1) * WIDE] = h.astype(BF)

    ways = (up_y, down_y)
    near = (yp, ym)

    class Along:
        def __init__(self, i, j):
            self.i, self.j = i, j

        def start(self):
            i, j = self.i, self.j
            self.opposite = [send(part.at[j, d, :, yo], ro.at[i, d], ways[d], "ro", i, d) for d in range(2)]
            self.arrive = [send(part.at[j, 1 - d, :, near[d]], ra.at[i, d, 1 - d], ways[d], "ra", i, d, 1 - d) for d in range(2)]

        def forward(self):
            i, j = self.i, self.j
            for d in range(2):
                self.opposite[d].wait_recv()
                add(part.at[j, d, :, near[d]], ro.at[i, d])
                self.arrive.append(send(part.at[j, d, :, near[d]], ra.at[i, d, d], ways[d], "ra", i, d, d))

        def gather(self):
            i, j = self.i, self.j
            for c in self.arrive:
                c.wait_recv()

            def total(m, x):
                return part[j, m, x, y].astype(F32) + ra[i, 0, m, x].astype(F32) + ra[i, 1, m, x].astype(F32)

            for m in range(2):
                fs[i, m] = total(m, xo).astype(BF)
            self.last = send(fs.at[i], fx.at[i], cross, "fx", i)
            for m in range(2):
                acc[i, m] = total(m, xm)

        def end(self):
            i, j = self.i, self.j
            self.last.wait_recv()
            finish(j, acc[i, 0] + fx[i, 0].astype(F32), acc[i, 1] + fx[i, 1].astype(F32))

    class Cross:
        def __init__(self, i, j):
            self.i, self.j = i, j

        def start(self):
            i, j = self.i, self.j
            self.first = send(part.at[j, :, xo], rx.at[i], cross, "rx", i)

        def turn(self):
            i, j = self.i, self.j
            self.first.wait_recv()
            for m in range(2):
                add(part.at[j, m, xm], rx.at[i, m])
            self.opposite = [send(part.at[j, d, xm, yo], qo.at[i, d], ways[d], "qo", i, d) for d in range(2)]
            self.arrive = [send(part.at[j, 1 - d, xm, near[d]], qa.at[i, d, 1 - d], ways[d], "qa", i, d, 1 - d) for d in range(2)]

        def forward(self):
            i, j = self.i, self.j
            for d in range(2):
                self.opposite[d].wait_recv()
                add(part.at[j, d, xm, near[d]], qo.at[i, d])
                self.arrive.append(send(part.at[j, d, xm, near[d]], qa.at[i, d, d], ways[d], "qa", i, d, d))

        def end(self):
            i, j = self.i, self.j
            for c in self.arrive:
                c.wait_recv()

            def total(m):
                return part[j, m, xm, y].astype(F32) + qa[i, 0, m].astype(F32) + qa[i, 1, m].astype(F32)

            finish(j, total(0), total(1))

    class Last:
        def start(self):
            self.opposite = [send(parts_last.at[d, yo], to.at[d], ways[d], "to", d) for d in range(2)]
            self.arrive = [send(parts_last.at[1 - d, near[d]], ta.at[d, 1 - d], ways[d], "ta", d, 1 - d) for d in range(2)]

        def forward(self):
            for d in range(2):
                self.opposite[d].wait_recv()
                add(parts_last.at[d, near[d]], to.at[d])
                self.arrive.append(send(parts_last.at[d, near[d]], ta.at[d, d], ways[d], "ta", d, d))

        def gather(self):
            for c in self.arrive:
                c.wait_recv()

            def total(x):
                return parts_last[x, y].astype(F32) + ta[0, x].astype(F32) + ta[1, x].astype(F32)

            ts[...] = total(xo).astype(BF)
            self.last = send(ts, tx, cross, "tx")
            tacc[...] = total(xm)

        def end(self):
            self.last.wait_recv()
            gate = tacc[...] + tx[...].astype(F32)
            up = pltpu.roll(gate, 64, 1)
            h = gate / (1 + jnp.exp(-gate)) * up
            hid[:, MAIN:FF] = h[:, 0:LAST].astype(BF)

    along = [Along(i, j) for i, j in enumerate(ALONG)]
    crossed = [Cross(i, j) for i, j in enumerate(CROSS)]
    last = Last()
    for j in range(CHUNKS):
        compute(j)
        (crossed[CROSS.index(j)] if j in CROSS else along[ALONG.index(j)]).start()
    compute_last()
    last.start()
    along[0].forward()
    along[1].forward()
    crossed[0].turn()
    along[2].forward()
    along[3].forward()
    last.forward()
    along[0].gather()
    crossed[0].forward()
    crossed[1].turn()
    along[1].gather()
    crossed[1].forward()
    along[2].gather()
    crossed[0].end()
    crossed[2].turn()
    along[3].gather()
    last.gather()
    crossed[2].forward()
    crossed[1].end()
    along[0].end()
    along[1].end()
    along[2].end()
    along[3].end()
    last.end()
    crossed[2].end()

    for c in sent:
        c.wait_send()
    for j in range(CHUNKS):
        swap(j).wait_send()

    @pl.when(even)
    def _():
        far.wait_send()
        for q in range(2):
            for d in range(2):
                hop(d, 1, q, z).wait_send()
                hop(d, 3, q, source(d, 2)).wait_send()

    @pl.when(jnp.logical_not(even))
    def _():
        t0.wait_send()
        for q in range(2):
            for d in range(2):
                hop(d, 2, q, source(d, 1)).wait_send()
                if d == q:
                    hop(d, 4, q, source(d, 3)).wait_send()

    store_g.wait()
    store_u.wait()
    assert len(names.names) <= COPIES, len(names.names)


COPIES = 160


def body(*args):
    vmem = pl.BlockSpec(memory_space=pltpu.VMEM)
    smem = pl.BlockSpec(memory_space=pltpu.SMEM)
    anywhere = pl.BlockSpec(memory_space=pl.ANY)
    n_a, n_c = len(ALONG), len(CROSS)

    def b(*shape):
        return pltpu.VMEM(shape, BF)

    def f(*shape):
        return pltpu.VMEM(shape, F32)

    scratch = [
        b(2, 4, ROWS, 2 * DEPTH),
        b(DEPTH, FF), b(DEPTH, FF), b(DEPTH, FF), b(DEPTH, FF),
        b(CHUNKS, 2, 2 * DEPTH, WIDE),
        b(2 * DEPTH, 128),
        f(2, DEPTH, 128),
        b(16, 2, 32, 128), b(15, 2, 32, 128), b(16, 2, 32, 128),
        b(2, 8, 16, FF), b(8, 16, FF), b(8, 16, FF), b(7, 16, FF), b(2, 8, 16, FF),
        b(CHUNKS, 2, 2, 4, ROWS, WIDE),
        b(2, 4, ROWS, 128),
        b(n_c, 2, 4, ROWS, WIDE), b(n_c, 2, ROWS, WIDE), b(n_c, 2, 2, ROWS, WIDE),
        b(n_a, 2, 2, ROWS, WIDE), b(n_a, 2, 2, 2, ROWS, WIDE),
        f(n_a, 2, ROWS, WIDE), b(n_a, 2, ROWS, WIDE), b(n_a, 2, ROWS, WIDE),
        b(2, ROWS, 128), b(2, 2, ROWS, 128), f(ROWS, 128), b(ROWS, 128), b(ROWS, 128),
        pltpu.SemaphoreType.DMA((COPIES,)), pltpu.SemaphoreType.DMA((COPIES,)), pltpu.SemaphoreType.DMA((4,)),
    ]
    return pl.pallas_call(
        kernel,
        out_shape=(
            jax.ShapeDtypeStruct((DEPTH, FF), BF),
            jax.ShapeDtypeStruct((DEPTH, FF), BF),
            jax.ShapeDtypeStruct((ROWS, FF), BF),
        ),
        in_specs=[vmem, anywhere, anywhere, vmem, vmem, vmem, vmem, smem, smem],
        out_specs=(anywhere, anywhere, vmem),
        scratch_shapes=scratch,
        compiler_params=pltpu.CompilerParams(
            collective_id=0, has_side_effects=True, vmem_limit_bytes=56 * 1024 * 1024
        ),
        cost_estimate=pl.CostEstimate(flops=7_000_000_000, bytes_accessed=10_000_000, transcendentals=200_000),
    )(*args)


def solution(mesh):
    return jax.shard_map(
        body,
        mesh=mesh,
        in_specs=(
            P("col", "row"),
            P("row", "col"),
            P("row", "col"),
            P("col", "row", None),
            P("col", "row", None),
            P("row", None, "col"),
            P("row", None, "col"),
            P(),
            P(),
        ),
        out_specs=(P("row", "col"), P("row", "col"), P("row", "col")),
        check_vma=False,
    )
```

```python
import jax
import jax.numpy as jnp
from jax import lax
from jax.experimental import pallas as pl
from jax.experimental.pallas import tpu as pltpu
from jax.sharding import PartitionSpec as P

MESH = pl.DeviceIdType.MESH
BF, F32 = jnp.bfloat16, jnp.float32
ROWS, DEPTH, FF, RANK = 96, 512, 1848, 64
WIDE, CHUNKS = 256, 7
MAIN = WIDE * CHUNKS
LAST = FF - MAIN
CROSS = (0, 2, 4)
ALONG = (1, 3, 5, 6)


class Semaphores:
    def __init__(self):
        self.names = {}

    def of(self, *name):
        return self.names.setdefault(name, len(self.names))


def kernel(
    tok, gw, uw, gl, ul, gu, uu, out_s, inc_s,
    vg, vu, hid,
    T, wg, wu, wc, wt, lc, l0, ls, lr, lf, uc, u0, us, ur, uf,
    part, parts_last, rx, qo, qa, ro, ra, acc, fs, fx, to, ta, tacc, ts, tx,
    ssem, rsem, lsem,
):
    row, col = lax.axis_index("row"), lax.axis_index("col")
    k, chip = row % 2, row // 2
    y, xm = row // 4, (row // 2) % 2
    xo = 1 - xm
    yp, yo, ym = (y + 1) % 4, (y + 2) % 4, (y + 3) % 4
    xh, z = col // 8, col % 8
    names = Semaphores()

    partner = (chip * 2 + 1 - k, col)
    cross = (y * 4 + xo * 2 + k, col)
    up_y = (yp * 4 + xm * 2 + k, col)
    down_y = (ym * 4 + xm * 2 + k, col)
    far_x = (row, (1 - xh) * 8 + z)
    up_z = (row, xh * 8 + (z + 1) % 8)
    down_z = (row, xh * 8 + (z + 7) % 8)

    def copy(src, dst, target, index):
        return pltpu.make_async_remote_copy(
            src_ref=src, dst_ref=dst, send_sem=ssem.at[index], recv_sem=rsem.at[index],
            device_id=target, device_id_type=MESH,
        )

    sent = []

    def send(src, dst, target, *name):
        c = copy(src, dst, target, names.of(*name))
        c.start()
        sent.append(c)
        return c

    load_g = pltpu.make_async_copy(gw, wg, lsem.at[0])
    load_u = pltpu.make_async_copy(uw, wu, lsem.at[1])
    load_g.start()
    load_u.start()

    barrier = pltpu.get_barrier_semaphore()
    pl.semaphore_signal(barrier, inc=1, device_id=partner, device_id_type=MESH)
    pl.semaphore_signal(barrier, inc=1, device_id=far_x, device_id_type=MESH)
    for i in range(1, 8):
        pl.semaphore_signal(barrier, inc=1, device_id=((chip + i) % 8 * 2 + k, col), device_id_type=MESH)
        pl.semaphore_signal(barrier, inc=1, device_id=(row, xh * 8 + (z + i) % 8), device_id_type=MESH)

    new, old = inc_s[0], out_s[0]
    for m, ref in enumerate((gu, uu)):
        b = ref[0]
        uc[m, 0:4] = jnp.where(new == row, b, jnp.zeros_like(b)).reshape(4, 16, FF)
        uc[m, 4:8] = jnp.where(old == row, -b, jnp.zeros_like(b)).reshape(4, 16, FF)
    for m, ref in enumerate((gl, ul)):
        a = ref[0]
        lc[8 * m:8 * m + 4] = jnp.where(new == col, a, jnp.zeros_like(a)).reshape(4, 16, DEPTH)
        lc[8 * m + 4:8 * m + 8] = jnp.where(old == col, a, jnp.zeros_like(a)).reshape(4, 16, DEPTH)
    pl.semaphore_wait(barrier, 16)

    even = k == z % 2
    odd = jnp.logical_not(even)
    xs, ys = (z // 2) % 2, col // 4
    t0 = [
        copy(tok.at[PART * p:PART * (p + 1)], T.at[xs, ys, PART * p:PART * (p + 1), DEPTH:], partner, names.of("t0", p))
        for p in range(PARTS)
    ]

    @pl.when(odd)
    def _():
        for c in t0:
            c.start()

    @pl.when(even)
    def _():
        T[xs, ys, :, 0:DEPTH] = tok[...]

    c_l0 = send(lc.at[pl.ds(8 * (1 - xh), 8)], l0, far_x, "l0")
    c_u0 = send(uc.at[1 - k], u0, partner, "u0")

    def block(zz, q, p):
        return T.at[(zz // 2) % 2, (xh + q) % 2 * 2 + zz // 4, PART * p:PART * (p + 1)]

    def hop(direction, stage, q, p, zz):
        target = (up_z, down_z)[direction]
        return copy(block(zz, q, p), block(zz, q, p), target, names.of("z", direction, stage, q, p))

    def source(direction, distance):
        return (z - distance + 8) % 8 if direction == 0 else (z + distance) % 8

    def far(p, q):
        return copy(block(z, q, p), block(z, q, p), far_x, names.of("h", p))

    def forward(stage, q):
        for p in range(PARTS):
            for d in range(2):
                hop(d, stage, q, p, source(d, stage)).wait_recv()
                if stage < 3 or d == q:
                    hop(d, stage + 1, q, p, source(d, stage)).start()

    @pl.when(even)
    def _():
        for p in range(PARTS):
            t0[p].wait_recv()
            for d in range(2):
                hop(d, 1, 0, p, z).start()
            far(p, 0).start()

    c_u0.wait_recv()
    us[...] = uc[k] + u0[...]
    u1 = [send(us.at[(chip + i) % 8], ur.at[i - 1], ((chip + i) % 8 * 2 + k, col), "u1", i) for i in range(1, 8)]

    @pl.when(odd)
    def _():
        forward(1, 0)

    c_l0.wait_recv()
    ls[...] = lc[pl.ds(8 * xh, 8)] + l0[...]
    l1 = [send(ls.at[(z + i) % 8], lr.at[i - 1], (row, xh * 8 + (z + i) % 8), "l1", i) for i in range(1, 8)]

    @pl.when(even)
    def _():
        for p in range(PARTS):
            far(p, 1).wait_recv()
            for d in range(2):
                hop(d, 1, 1, p, z).start()
        forward(2, 0)

    @pl.when(odd)
    def _():
        forward(1, 1)

    for c in l1:
        c.wait_recv()
    total = ls[z].astype(F32)
    for i in range(7):
        total = total + lr[i].astype(F32)
    mine = col
    lf[mine] = total.astype(BF)
    l2 = [send(lf.at[mine], lf.at[mine], (row, xh * 8 + (z + i) % 8), "l2", i) for i in range(1, 8)]
    l3 = [send(lf.at[mine], lf.at[mine], far_x, "l3", 0)]

    for c in u1:
        c.wait_recv()
    total = us[chip].astype(F32)
    for i in range(7):
        total = total + ur[i].astype(F32)
    uf[k, chip] = total.astype(BF)
    u2 = [send(uf.at[k, chip], uf.at[k, chip], ((chip + i) % 8 * 2 + k, col), "u2", i) for i in range(1, 8)]
    u3 = [send(uf.at[k, chip], uf.at[k, chip], partner, "u3", 0)]

    @pl.when(odd)
    def _():
        forward(3, 0)

    @pl.when(even)
    def _():
        forward(2, 1)

    for i in range(1, 8):
        l2[i - 1].wait_recv()
        s = xh * 8 + (z - i + 8) % 8
        l3.append(send(lf.at[s], lf.at[s], far_x, "l3", i))

    @pl.when(odd)
    def _():
        forward(3, 1)

    for i in range(1, 8):
        u2[i - 1].wait_recv()
        s = (chip - i + 8) % 8
        u3.append(send(uf.at[k, s], uf.at[k, s], partner, "u3", i))

    for c in l3:
        c.wait_recv()
    for c in u3:
        c.wait_recv()
    load_g.wait()
    load_u.wait()

    def swap(j):
        return copy(wc.at[j, :, :, 0:DEPTH], wc.at[j, :, :, DEPTH:], partner, first_swap + j)

    for j in range(CHUNKS):
        index = names.of("w", j)
        if j == 0:
            first_swap = index

    def merged(w, m, cols):
        delta = lax.dot_general(
            uf[m, :, :, cols].reshape(2 * RANK, -1), lf[8 * m:8 * m + 8].reshape(2 * RANK, DEPTH),
            (((0,), (0,)), ((), ())), preferred_element_type=F32,
        )
        return (w[cols].astype(F32) + delta).astype(BF)

    def merge(j, carry):
        cols = pl.ds(pl.multiple_of(j * WIDE, WIDE), WIDE)
        for m, (w, v) in enumerate(((wg, vg), (wu, vu))):
            piece = merged(w, m, cols)
            v[cols] = piece
            wc[j, m, :, 0:DEPTH] = piece
        swap(j).start()
        return carry

    lax.fori_loop(0, CHUNKS, merge, 0)
    wt[:, 0:DEPTH] = jnp.zeros((128, DEPTH), BF)
    for m, (w, v) in enumerate(((wg, vg), (wu, vu))):
        piece = merged(w, m, slice(MAIN, FF))
        v[MAIN:FF] = piece
        wt[64 * m:64 * m + LAST, 0:DEPTH] = piece
    c_wt = send(wt.at[:, 0:DEPTH], wt.at[:, DEPTH:], partner, "wt")
    @pl.when(even)
    def _():
        for p in range(PARTS):
            for d in range(2):
                hop(d, 4, d, p, source(d, 4)).wait_recv()

    def times(x, w):
        return lax.dot_general(
            T[x].reshape(4 * ROWS, 2 * DEPTH), w, (((1,), (1,)), ((), ())), preferred_element_type=F32
        )

    def compute(j):
        swap(j).wait_recv()

        def quarter(i, carry):
            m, x = i // 2, i % 2
            p = times(x, wc[j, m])
            part[j, m, x] = p.astype(BF).reshape(4, ROWS, WIDE)
            return carry

        lax.fori_loop(0, 4, quarter, 0)

    def compute_last():
        c_wt.wait_recv()
        for x in range(2):
            p = times(x, wt[...])
            parts_last[x] = p.astype(BF).reshape(4, ROWS, 128)

    def add(ref, other):
        ref[...] = (ref[...].astype(F32) + other[...].astype(F32)).astype(BF)

    def finish(j, gate, up):
        h = gate / (1 + jnp.exp(-gate)) * up
        hid[:, j * WIDE:(j + 1) * WIDE] = h.astype(BF)

    ways = (up_y, down_y)
    near = (yp, ym)

    class Along:
        def __init__(self, i, j):
            self.i, self.j = i, j

        def start(self):
            i, j = self.i, self.j
            self.opposite = [send(part.at[j, d, :, yo], ro.at[i, d], ways[d], "ro", i, d) for d in range(2)]
            self.arrive = [send(part.at[j, 1 - d, :, near[d]], ra.at[i, d, 1 - d], ways[d], "ra", i, d, 1 - d) for d in range(2)]

        def forward(self):
            i, j = self.i, self.j
            for d in range(2):
                self.opposite[d].wait_recv()
                add(part.at[j, d, :, near[d]], ro.at[i, d])
                self.arrive.append(send(part.at[j, d, :, near[d]], ra.at[i, d, d], ways[d], "ra", i, d, d))

        def gather(self):
            i, j = self.i, self.j
            for c in self.arrive:
                c.wait_recv()

            def total(m, x):
                return part[j, m, x, y].astype(F32) + ra[i, 0, m, x].astype(F32) + ra[i, 1, m, x].astype(F32)

            for m in range(2):
                fs[i, m] = total(m, xo).astype(BF)
            self.last = send(fs.at[i], fx.at[i], cross, "fx", i)
            for m in range(2):
                acc[i, m] = total(m, xm)

        def end(self):
            i, j = self.i, self.j
            self.last.wait_recv()
            finish(j, acc[i, 0] + fx[i, 0].astype(F32), acc[i, 1] + fx[i, 1].astype(F32))

    class Cross:
        def __init__(self, i, j):
            self.i, self.j = i, j

        def start(self):
            i, j = self.i, self.j
            self.first = send(part.at[j, :, xo], rx.at[i], cross, "rx", i)

        def turn(self):
            i, j = self.i, self.j
            self.first.wait_recv()
            for m in range(2):
                add(part.at[j, m, xm], rx.at[i, m])
            self.opposite = [send(part.at[j, d, xm, yo], qo.at[i, d], ways[d], "qo", i, d) for d in range(2)]
            self.arrive = [send(part.at[j, 1 - d, xm, near[d]], qa.at[i, d, 1 - d], ways[d], "qa", i, d, 1 - d) for d in range(2)]

        def forward(self):
            i, j = self.i, self.j
            for d in range(2):
                self.opposite[d].wait_recv()
                add(part.at[j, d, xm, near[d]], qo.at[i, d])
                self.arrive.append(send(part.at[j, d, xm, near[d]], qa.at[i, d, d], ways[d], "qa", i, d, d))

        def end(self):
            i, j = self.i, self.j
            for c in self.arrive:
                c.wait_recv()

            def total(m):
                return part[j, m, xm, y].astype(F32) + qa[i, 0, m].astype(F32) + qa[i, 1, m].astype(F32)

            finish(j, total(0), total(1))

    class Last:
        def start(self):
            self.opposite = [send(parts_last.at[d, yo], to.at[d], ways[d], "to", d) for d in range(2)]
            self.arrive = [send(parts_last.at[1 - d, near[d]], ta.at[d, 1 - d], ways[d], "ta", d, 1 - d) for d in range(2)]

        def forward(self):
            for d in range(2):
                self.opposite[d].wait_recv()
                add(parts_last.at[d, near[d]], to.at[d])
                self.arrive.append(send(parts_last.at[d, near[d]], ta.at[d, d], ways[d], "ta", d, d))

        def gather(self):
            for c in self.arrive:
                c.wait_recv()

            def total(x):
                return parts_last[x, y].astype(F32) + ta[0, x].astype(F32) + ta[1, x].astype(F32)

            ts[...] = total(xo).astype(BF)
            self.last = send(ts, tx, cross, "tx")
            tacc[...] = total(xm)

        def end(self):
            self.last.wait_recv()
            gate = tacc[...] + tx[...].astype(F32)
            up = pltpu.roll(gate, 64, 1)
            h = gate / (1 + jnp.exp(-gate)) * up
            hid[:, MAIN:FF] = h[:, 0:LAST].astype(BF)

    along = [Along(i, j) for i, j in enumerate(ALONG)]
    crossed = [Cross(i, j) for i, j in enumerate(CROSS)]
    last = Last()
    for j in range(CHUNKS):
        compute(j)
        (crossed[CROSS.index(j)] if j in CROSS else along[ALONG.index(j)]).start()
    compute_last()
    last.start()
    along[0].forward()
    along[1].forward()
    crossed[0].turn()
    along[2].forward()
    along[3].forward()
    last.forward()
    along[0].gather()
    crossed[0].forward()
    crossed[1].turn()
    along[1].gather()
    crossed[1].forward()
    along[2].gather()
    crossed[0].end()
    crossed[2].turn()
    along[3].gather()
    last.gather()
    crossed[2].forward()
    crossed[1].end()
    along[0].end()
    along[1].end()
    along[2].end()
    along[3].end()
    last.end()
    crossed[2].end()

    for c in sent:
        c.wait_send()
    for j in range(CHUNKS):
        swap(j).wait_send()

    @pl.when(even)
    def _():
        for p in range(PARTS):
            far(p, 0).wait_send()
            for q in range(2):
                for d in range(2):
                    hop(d, 1, q, p, z).wait_send()
                    hop(d, 3, q, p, source(d, 2)).wait_send()

    @pl.when(odd)
    def _():
        for p in range(PARTS):
            t0[p].wait_send()
            for q in range(2):
                for d in range(2):
                    hop(d, 2, q, p, source(d, 1)).wait_send()
                    if d == q:
                        hop(d, 4, q, p, source(d, 3)).wait_send()

    assert len(names.names) <= COPIES, len(names.names)


COPIES = 192
PARTS = 3
PART = ROWS // PARTS


def body(tokens, gate_weight, up_weight, gate_lower, up_lower, *others):
    args = (
        tokens, gate_weight.T, up_weight.T, gate_lower.swapaxes(1, 2), up_lower.swapaxes(1, 2), *others
    )
    vmem = pl.BlockSpec(memory_space=pltpu.VMEM)
    smem = pl.BlockSpec(memory_space=pltpu.SMEM)
    anywhere = pl.BlockSpec(memory_space=pl.ANY)
    n_a, n_c = len(ALONG), len(CROSS)

    def b(*shape):
        return pltpu.VMEM(shape, BF)

    def f(*shape):
        return pltpu.VMEM(shape, F32)

    scratch = [
        b(2, 4, ROWS, 2 * DEPTH),
        b(FF, DEPTH), b(FF, DEPTH),
        b(CHUNKS, 2, WIDE, 2 * DEPTH),
        b(128, 2 * DEPTH),
        b(16, 16, DEPTH), b(8, 16, DEPTH), b(8, 16, DEPTH), b(7, 16, DEPTH), b(16, 16, DEPTH),
        b(2, 8, 16, FF), b(8, 16, FF), b(8, 16, FF), b(7, 16, FF), b(2, 8, 16, FF),
        b(CHUNKS, 2, 2, 4, ROWS, WIDE),
        b(2, 4, ROWS, 128),
        b(n_c, 2, 4, ROWS, WIDE), b(n_c, 2, ROWS, WIDE), b(n_c, 2, 2, ROWS, WIDE),
        b(n_a, 2, 2, ROWS, WIDE), b(n_a, 2, 2, 2, ROWS, WIDE),
        f(n_a, 2, ROWS, WIDE), b(n_a, 2, ROWS, WIDE), b(n_a, 2, ROWS, WIDE),
        b(2, ROWS, 128), b(2, 2, ROWS, 128), f(ROWS, 128), b(ROWS, 128), b(ROWS, 128),
        pltpu.SemaphoreType.DMA((COPIES,)), pltpu.SemaphoreType.DMA((COPIES,)), pltpu.SemaphoreType.DMA((4,)),
    ]
    new_gate, new_up, hidden = pl.pallas_call(
        kernel,
        out_shape=(
            pltpu.VMEM((FF, DEPTH), BF),
            pltpu.VMEM((FF, DEPTH), BF),
            pltpu.VMEM((ROWS, FF), BF),
        ),
        in_specs=[vmem, anywhere, anywhere, vmem, vmem, vmem, vmem, smem, smem],
        out_specs=(vmem, vmem, vmem),
        scratch_shapes=scratch,
        compiler_params=pltpu.CompilerParams(
            collective_id=0, has_side_effects=True, vmem_limit_bytes=56 * 1024 * 1024
        ),
        cost_estimate=pl.CostEstimate(flops=7_000_000_000, bytes_accessed=10_000_000, transcendentals=200_000),
    )(*args)
    return new_gate.T, new_up.T, hidden


def solution(mesh):
    return jax.shard_map(
        body,
        mesh=mesh,
        in_specs=(
            P("col", "row"),
            P("row", "col"),
            P("row", "col"),
            P("col", "row", None),
            P("col", "row", None),
            P("row", None, "col"),
            P("row", None, "col"),
            P(),
            P(),
        ),
        out_specs=(P("row", "col"), P("row", "col"), P("row", "col")),
        check_vma=False,
    )
```

```python
import jax
import jax.numpy as jnp
from jax import lax
from jax.experimental import pallas as pl
from jax.experimental.pallas import tpu as pltpu
from jax.sharding import PartitionSpec as P

MESH = pl.DeviceIdType.MESH
BF, F32 = jnp.bfloat16, jnp.float32
ROWS, DEPTH, FF, RANK = 96, 512, 1848, 64
WIDE, CHUNKS = 256, 7
MAIN = WIDE * CHUNKS
LAST = FF - MAIN
CROSS = (1, 3, 5)
ALONG = (0, 2, 4, 6)


class Semaphores:
    def __init__(self):
        self.names = {}

    def of(self, *name):
        return self.names.setdefault(name, len(self.names))


def kernel(
    tok_in, gw, uw, gl_in, ul_in, gu_in, uu_in, out_s, inc_s,
    vg, vu, hid,
    tok, gl, ul, gu, uu, T, wg, wu, wc, wt, lc, l0, ls, lr, lf, uc, u0, us, ur, uq, ux, uf,
    part, parts_last, rx, qo, qa, ro, ra, acc, fs, fx, to, ta, tacc, ts, tx,
    ssem, rsem, lsem,
):
    row, col = lax.axis_index("row"), lax.axis_index("col")
    k, chip = row % 2, row // 2
    y, xm = row // 4, (row // 2) % 2
    xo = 1 - xm
    yp, yo, ym = (y + 1) % 4, (y + 2) % 4, (y + 3) % 4
    xh, z = col // 8, col % 8
    names = Semaphores()

    partner = (chip * 2 + 1 - k, col)
    cross = (y * 4 + xo * 2 + k, col)
    up_y = (yp * 4 + xm * 2 + k, col)
    down_y = (ym * 4 + xm * 2 + k, col)
    far_x = (row, (1 - xh) * 8 + z)
    far_partner = (chip * 2 + 1 - k, (1 - xh) * 8 + z)
    up_z = (row, xh * 8 + (z + 1) % 8)
    down_z = (row, xh * 8 + (z + 7) % 8)

    def ring_y(i):
        return ((y + i) % 4 * 4 + xm * 2 + k, col)

    def copy(src, dst, target, index):
        return pltpu.make_async_remote_copy(
            src_ref=src, dst_ref=dst, send_sem=ssem.at[index], recv_sem=rsem.at[index],
            device_id=target, device_id_type=MESH,
        )

    sent = []

    def send(src, dst, target, *name):
        c = copy(src, dst, target, names.of(*name))
        c.start()
        sent.append(c)
        return c

    barrier = pltpu.get_barrier_semaphore()
    pl.semaphore_signal(barrier, inc=1, device_id=partner, device_id_type=MESH)
    pl.semaphore_signal(barrier, inc=1, device_id=far_x, device_id_type=MESH)
    pl.semaphore_signal(barrier, inc=1, device_id=far_partner, device_id_type=MESH)
    pl.semaphore_signal(barrier, inc=1, device_id=cross, device_id_type=MESH)
    for i in range(1, 4):
        pl.semaphore_signal(barrier, inc=1, device_id=ring_y(i), device_id_type=MESH)
    for i in range(1, 8):
        pl.semaphore_signal(barrier, inc=1, device_id=(row, xh * 8 + (z + i) % 8), device_id_type=MESH)

    loads = [
        pltpu.make_async_copy(src, dst, lsem.at[2 + i])
        for i, (src, dst) in enumerate(((gu_in, gu), (uu_in, uu), (gl_in, gl), (ul_in, ul), (tok_in, tok)))
    ]
    for c in loads:
        c.start()
    load_g = pltpu.make_async_copy(gw, wg, lsem.at[0])
    load_u = pltpu.make_async_copy(uw, wu, lsem.at[1])
    load_g.start()
    load_u.start()

    for c in loads:
        c.wait()
    new, old = inc_s[0], out_s[0]
    for m, ref in enumerate((gu, uu)):
        b = ref[0]
        uc[m, 0:4] = jnp.where(new == row, b, jnp.zeros_like(b)).reshape(4, 16, FF)
        uc[m, 4:8] = jnp.where(old == row, -b, jnp.zeros_like(b)).reshape(4, 16, FF)
    for m, ref in enumerate((gl, ul)):
        a = ref[0]
        lc[8 * m:8 * m + 4] = jnp.where(new == col, a, jnp.zeros_like(a)).reshape(4, 16, DEPTH)
        lc[8 * m + 4:8 * m + 8] = jnp.where(old == col, a, jnp.zeros_like(a)).reshape(4, 16, DEPTH)
    pl.semaphore_wait(barrier, 14)

    even = k == z % 2
    odd = jnp.logical_not(even)
    xs, ys = (z // 2) % 2, col // 4
    t0 = [
        copy(tok.at[PART * p:PART * (p + 1)], T.at[xs, ys, PART * p:PART * (p + 1), DEPTH:], partner, names.of("t0", p))
        for p in range(PARTS)
    ]


    def far(p, half, place):
        rows = slice(PART * p, PART * (p + 1))
        dst = T.at[xs, place, rows, DEPTH * half:DEPTH * (half + 1)]
        return copy(tok.at[rows], dst, (far_x, far_partner)[half], names.of("h", p, half))

    @pl.when(odd)
    def _():
        for p in range(PARTS):
            t0[p].start()
        for p in range(PARTS):
            far(p, 1, ys).start()

    @pl.when(even)
    def _():
        for p in range(PARTS):
            far(p, 0, ys).start()
        T[xs, ys, :, 0:DEPTH] = tok[...]

    c_u0 = send(uc.at[1 - k], u0, partner, "u0")
    c_l0 = send(lc.at[pl.ds(8 * (1 - xh), 8)], l0, far_x, "l0")

    def block(zz, q, p):
        return T.at[(zz // 2) % 2, (xh + q) % 2 * 2 + zz // 4, PART * p:PART * (p + 1)]

    def hop(direction, stage, q, p, zz):
        target = (up_z, down_z)[direction]
        return copy(block(zz, q, p), block(zz, q, p), target, names.of("z", direction, stage, q, p))

    def source(direction, distance):
        return (z - distance + 8) % 8 if direction == 0 else (z + distance) % 8

    def forward(stage, q):
        for p in range(PARTS):
            for d in range(2):
                hop(d, stage, q, p, source(d, stage)).wait_recv()
                if stage < 3 or d == q:
                    hop(d, stage + 1, q, p, source(d, stage)).start()

    @pl.when(even)
    def _():
        for p in range(PARTS):
            t0[p].wait_recv()
            for d in range(2):
                hop(d, 1, 0, p, z).start()

    c_u0.wait_recv()
    us[...] = uc[k] + u0[...]
    u1 = [send(us.at[pl.ds((y + i) % 4 * 2, 2)], ur.at[i - 1], ring_y(i), "u1", i) for i in range(1, 4)]

    @pl.when(odd)
    def _():
        forward(1, 0)

    c_l0.wait_recv()
    ls[...] = lc[pl.ds(8 * xh, 8)] + l0[...]
    l1 = [send(ls.at[(z + i) % 8], lr.at[i - 1], (row, xh * 8 + (z + i) % 8), "l1", i) for i in range(1, 8)]

    @pl.when(even)
    def _():
        for p in range(PARTS):
            for half in range(2):
                far(p, half, (ys + 2) % 4).wait_recv()
            for d in range(2):
                hop(d, 1, 1, p, z).start()
        forward(2, 0)

    @pl.when(odd)
    def _():
        forward(1, 1)

    for c in u1:
        c.wait_recv()
    total = us[pl.ds(2 * y, 2)].astype(F32)
    for i in range(3):
        total = total + ur[i].astype(F32)
    uq[...] = total.astype(BF)
    c_ux = send(uq.at[xo], ux, cross, "ux")

    for c in l1:
        c.wait_recv()
    total = ls[z].astype(F32)
    for i in range(7):
        total = total + lr[i].astype(F32)
    mine = col
    lf[mine] = total.astype(BF)
    l2 = [send(lf.at[mine], lf.at[mine], (row, xh * 8 + (z + i) % 8), "l2", i) for i in range(1, 8)]
    l3 = [send(lf.at[mine], lf.at[mine], far_x, "l3", 0)]

    c_ux.wait_recv()
    uf[k, chip] = uq[xm] + ux[...]
    c_ua = send(uf.at[k, chip], uf.at[k, chip], cross, "ua")
    u2 = [send(uf.at[k, chip], uf.at[k, chip], ring_y(i), "u2", i) for i in range(1, 4)]
    u3 = [send(uf.at[k, chip], uf.at[k, chip], partner, "u3", 0)]

    @pl.when(odd)
    def _():
        forward(3, 0)

    beside = 2 * y + xo
    c_ua.wait_recv()
    u2b = [send(uf.at[k, beside], uf.at[k, beside], ring_y(i), "u2b", i) for i in range(1, 4)]
    u3.append(send(uf.at[k, beside], uf.at[k, beside], partner, "u3", 4))

    @pl.when(even)
    def _():
        forward(2, 1)

    for i in range(1, 8):
        l2[i - 1].wait_recv()
        s = xh * 8 + (z - i + 8) % 8
        l3.append(send(lf.at[s], lf.at[s], far_x, "l3", i))

    @pl.when(odd)
    def _():
        forward(3, 1)

    for i in range(1, 4):
        u2[i - 1].wait_recv()
        s = (y - i + 4) % 4 * 2 + xm
        u3.append(send(uf.at[k, s], uf.at[k, s], partner, "u3", i))
    for i in range(1, 4):
        u2b[i - 1].wait_recv()
        s = (y - i + 4) % 4 * 2 + xo
        u3.append(send(uf.at[k, s], uf.at[k, s], partner, "u3", 4 + i))

    for c in l3:
        c.wait_recv()
    for c in u3:
        c.wait_recv()
    load_g.wait()
    load_u.wait()

    def swap(j):
        return copy(wc.at[j, :, :, 0:DEPTH], wc.at[j, :, :, DEPTH:], partner, first_swap + j)

    for j in range(CHUNKS):
        index = names.of("w", j)
        if j == 0:
            first_swap = index

    def merged(w, m, cols):
        delta = lax.dot_general(
            uf[m, :, :, cols].reshape(2 * RANK, -1), lf[8 * m:8 * m + 8].reshape(2 * RANK, DEPTH),
            (((0,), (0,)), ((), ())), preferred_element_type=F32,
        )
        return (w[cols].astype(F32) + delta).astype(BF)

    def merge(j, carry):
        cols = pl.ds(pl.multiple_of(j * WIDE, WIDE), WIDE)
        for m, (w, v) in enumerate(((wg, vg), (wu, vu))):
            piece = merged(w, m, cols)
            v[cols] = piece
            wc[j, m, :, 0:DEPTH] = piece
        swap(j).start()
        return carry

    def merge_last():
        wt[:, 0:DEPTH] = jnp.zeros((128, DEPTH), BF)
        for m, (w, v) in enumerate(((wg, vg), (wu, vu))):
            piece = merged(w, m, slice(MAIN, FF))
            v[MAIN:FF] = piece
            wt[64 * m:64 * m + LAST, 0:DEPTH] = piece
        return send(wt.at[:, 0:DEPTH], wt.at[:, DEPTH:], partner, "wt")

    lax.fori_loop(0, AHEAD, merge, 0)

    @pl.when(even)
    def _():
        for p in range(PARTS):
            for d in range(2):
                hop(d, 4, d, p, source(d, 4)).wait_recv()

    def times(x, w):
        return lax.dot_general(
            T[x].reshape(4 * ROWS, 2 * DEPTH), w, (((1,), (1,)), ((), ())), preferred_element_type=F32
        )

    def compute(j):
        swap(j).wait_recv()

        def quarter(i, carry):
            m, x = i // 2, i % 2
            p = times(x, wc[j, m])
            part[j, m, x] = p.astype(BF).reshape(4, ROWS, WIDE)
            return carry

        lax.fori_loop(0, 4, quarter, 0)

    def compute_last(c_wt):
        c_wt.wait_recv()
        for x in range(2):
            p = times(x, wt[...])
            parts_last[x] = p.astype(BF).reshape(4, ROWS, 128)

    def add(ref, other):
        ref[...] = (ref[...].astype(F32) + other[...].astype(F32)).astype(BF)

    def finish(j, gate, up):
        h = gate / (1 + jnp.exp(-gate)) * up
        hid[:, j * WIDE:(j + 1) * WIDE] = h.astype(BF)

    ways = (up_y, down_y)
    near = (yp, ym)

    class Along:
        def __init__(self, i, j):
            self.i, self.j = i, j

        def start(self):
            i, j = self.i, self.j
            self.opposite = [send(part.at[j, d, :, yo], ro.at[i, d], ways[d], "ro", i, d) for d in range(2)]
            self.arrive = [send(part.at[j, 1 - d, :, near[d]], ra.at[i, d, 1 - d], ways[d], "ra", i, d, 1 - d) for d in range(2)]

        def forward(self):
            i, j = self.i, self.j
            for d in range(2):
                self.opposite[d].wait_recv()
                add(part.at[j, d, :, near[d]], ro.at[i, d])
                self.arrive.append(send(part.at[j, d, :, near[d]], ra.at[i, d, d], ways[d], "ra", i, d, d))

        def gather(self):
            i, j = self.i, self.j
            for c in self.arrive:
                c.wait_recv()

            def total(m, x):
                return part[j, m, x, y].astype(F32) + ra[i, 0, m, x].astype(F32) + ra[i, 1, m, x].astype(F32)

            for m in range(2):
                fs[i, m] = total(m, xo).astype(BF)
            self.last = send(fs.at[i], fx.at[i], cross, "fx", i)
            for m in range(2):
                acc[i, m] = total(m, xm)

        def end(self):
            i, j = self.i, self.j
            self.last.wait_recv()
            finish(j, acc[i, 0] + fx[i, 0].astype(F32), acc[i, 1] + fx[i, 1].astype(F32))

    class Cross:
        def __init__(self, i, j):
            self.i, self.j = i, j

        def start(self):
            i, j = self.i, self.j
            self.first = send(part.at[j, :, xo], rx.at[i], cross, "rx", i)

        def turn(self):
            i, j = self.i, self.j
            self.first.wait_recv()
            for m in range(2):
                add(part.at[j, m, xm], rx.at[i, m])
            self.opposite = [send(part.at[j, d, xm, yo], qo.at[i, d], ways[d], "qo", i, d) for d in range(2)]
            self.arrive = [send(part.at[j, 1 - d, xm, near[d]], qa.at[i, d, 1 - d], ways[d], "qa", i, d, 1 - d) for d in range(2)]

        def forward(self):
            i, j = self.i, self.j
            for d in range(2):
                self.opposite[d].wait_recv()
                add(part.at[j, d, xm, near[d]], qo.at[i, d])
                self.arrive.append(send(part.at[j, d, xm, near[d]], qa.at[i, d, d], ways[d], "qa", i, d, d))

        def end(self):
            i, j = self.i, self.j
            for c in self.arrive:
                c.wait_recv()

            def total(m):
                return part[j, m, xm, y].astype(F32) + qa[i, 0, m].astype(F32) + qa[i, 1, m].astype(F32)

            finish(j, total(0), total(1))

    class Last:
        def start(self):
            self.opposite = [send(parts_last.at[d, yo], to.at[d], ways[d], "to", d) for d in range(2)]
            self.arrive = [send(parts_last.at[1 - d, near[d]], ta.at[d, 1 - d], ways[d], "ta", d, 1 - d) for d in range(2)]

        def forward(self):
            for d in range(2):
                self.opposite[d].wait_recv()
                add(parts_last.at[d, near[d]], to.at[d])
                self.arrive.append(send(parts_last.at[d, near[d]], ta.at[d, d], ways[d], "ta", d, d))

        def gather(self):
            for c in self.arrive:
                c.wait_recv()

            def total(x):
                return parts_last[x, y].astype(F32) + ta[0, x].astype(F32) + ta[1, x].astype(F32)

            ts[...] = total(xo).astype(BF)
            self.last = send(ts, tx, cross, "tx")
            tacc[...] = total(xm)

        def end(self):
            self.last.wait_recv()
            gate = tacc[...] + tx[...].astype(F32)
            up = pltpu.roll(gate, 64, 1)
            h = gate / (1 + jnp.exp(-gate)) * up
            hid[:, MAIN:FF] = h[:, 0:LAST].astype(BF)

    along = [Along(i, j) for i, j in enumerate(ALONG)]
    crossed = [Cross(i, j) for i, j in enumerate(CROSS)]
    last = Last()
    for j in range(CHUNKS):
        compute(j)
        (crossed[CROSS.index(j)] if j in CROSS else along[ALONG.index(j)]).start()
        if j + AHEAD < CHUNKS:
            merge(j + AHEAD, 0)
        elif j + AHEAD == CHUNKS:
            c_wt = merge_last()
    compute_last(c_wt)
    last.start()
    along[0].forward()
    along[1].forward()
    crossed[0].turn()
    along[2].forward()
    along[3].forward()
    last.forward()
    along[0].gather()
    crossed[0].forward()
    crossed[1].turn()
    along[1].gather()
    crossed[1].forward()
    along[2].gather()
    crossed[0].end()
    crossed[2].turn()
    along[3].gather()
    last.gather()
    crossed[2].forward()
    crossed[1].end()
    along[0].end()
    along[1].end()
    along[2].end()
    along[3].end()
    last.end()
    crossed[2].end()

    for c in sent:
        c.wait_send()
    for j in range(CHUNKS):
        swap(j).wait_send()

    @pl.when(even)
    def _():
        for p in range(PARTS):
            far(p, 0, ys).wait_send()
            for q in range(2):
                for d in range(2):
                    hop(d, 1, q, p, z).wait_send()
                    hop(d, 3, q, p, source(d, 2)).wait_send()

    @pl.when(odd)
    def _():
        for p in range(PARTS):
            t0[p].wait_send()
            far(p, 1, ys).wait_send()
            for q in range(2):
                for d in range(2):
                    hop(d, 2, q, p, source(d, 1)).wait_send()
                    if d == q:
                        hop(d, 4, q, p, source(d, 3)).wait_send()

    assert len(names.names) <= COPIES, len(names.names)


def store(a, b, c, x, y, z, sems):
    copies = [
        pltpu.make_async_copy(src, dst, sems.at[i]) for i, (src, dst) in enumerate(((a, x), (b, y), (c, z)))
    ]
    for c in copies:
        c.start()
    for c in copies:
        c.wait()


COPIES = 192
PARTS = 3
AHEAD = 2
PART = ROWS // PARTS


def body(tokens, gate_weight, up_weight, gate_lower, up_lower, *others):
    args = (
        tokens, gate_weight.T, up_weight.T, gate_lower.swapaxes(1, 2), up_lower.swapaxes(1, 2), *others
    )
    vmem = pl.BlockSpec(memory_space=pltpu.VMEM)
    smem = pl.BlockSpec(memory_space=pltpu.SMEM)
    anywhere = pl.BlockSpec(memory_space=pl.ANY)
    n_a, n_c = len(ALONG), len(CROSS)

    def b(*shape):
        return pltpu.VMEM(shape, BF)

    def f(*shape):
        return pltpu.VMEM(shape, F32)

    scratch = [
        b(ROWS, DEPTH), b(1, RANK, DEPTH), b(1, RANK, DEPTH), b(1, RANK, FF), b(1, RANK, FF),
        b(2, 4, ROWS, 2 * DEPTH),
        b(FF, DEPTH), b(FF, DEPTH),
        b(CHUNKS, 2, WIDE, 2 * DEPTH),
        b(128, 2 * DEPTH),
        b(16, 16, DEPTH), b(8, 16, DEPTH), b(8, 16, DEPTH), b(7, 16, DEPTH), b(16, 16, DEPTH),
        b(2, 8, 16, FF), b(8, 16, FF), b(8, 16, FF), b(3, 2, 16, FF), b(2, 16, FF), b(16, FF), b(2, 8, 16, FF),
        b(CHUNKS, 2, 2, 4, ROWS, WIDE),
        b(2, 4, ROWS, 128),
        b(n_c, 2, 4, ROWS, WIDE), b(n_c, 2, ROWS, WIDE), b(n_c, 2, 2, ROWS, WIDE),
        b(n_a, 2, 2, ROWS, WIDE), b(n_a, 2, 2, 2, ROWS, WIDE),
        f(n_a, 2, ROWS, WIDE), b(n_a, 2, ROWS, WIDE), b(n_a, 2, ROWS, WIDE),
        b(2, ROWS, 128), b(2, 2, ROWS, 128), f(ROWS, 128), b(ROWS, 128), b(ROWS, 128),
        pltpu.SemaphoreType.DMA((COPIES,)), pltpu.SemaphoreType.DMA((COPIES,)), pltpu.SemaphoreType.DMA((7,)),
    ]
    new_gate, new_up, hidden = pl.pallas_call(
        kernel,
        out_shape=(
            pltpu.VMEM((FF, DEPTH), BF),
            pltpu.VMEM((FF, DEPTH), BF),
            pltpu.VMEM((ROWS, FF), BF),
        ),
        in_specs=[anywhere] * 7 + [smem] * 2,
        out_specs=(vmem, vmem, vmem),
        scratch_shapes=scratch,
        compiler_params=pltpu.CompilerParams(
            collective_id=0, has_side_effects=True, vmem_limit_bytes=56 * 1024 * 1024
        ),
        cost_estimate=pl.CostEstimate(flops=7_000_000_000, bytes_accessed=10_000_000, transcendentals=200_000),
    )(*args)
    new_gate, new_up, hidden = pl.pallas_call(
        store,
        out_shape=(
            jax.ShapeDtypeStruct((FF, DEPTH), BF),
            jax.ShapeDtypeStruct((FF, DEPTH), BF),
            jax.ShapeDtypeStruct((ROWS, FF), BF),
        ),
        in_specs=[anywhere] * 3,
        out_specs=(anywhere,) * 3,
        scratch_shapes=[pltpu.SemaphoreType.DMA((3,))],
        compiler_params=pltpu.CompilerParams(vmem_limit_bytes=1024 * 1024),
    )(new_gate, new_up, hidden)
    return new_gate.T, new_up.T, hidden


def solution(mesh):
    return jax.shard_map(
        body,
        mesh=mesh,
        in_specs=(
            P("col", "row"),
            P("row", "col"),
            P("row", "col"),
            P("col", "row", None),
            P("col", "row", None),
            P("row", None, "col"),
            P("row", None, "col"),
            P(),
            P(),
        ),
        out_specs=(P("row", "col"), P("row", "col"), P("row", "col")),
        check_vma=False,
    )
```

```python
import jax
import jax.numpy as jnp
from jax import lax
from jax.experimental import pallas as pl
from jax.experimental.pallas import tpu as pltpu
from jax.sharding import PartitionSpec as P

MESH = pl.DeviceIdType.MESH
BF, F32 = jnp.bfloat16, jnp.float32
ROWS, DEPTH, FF, RANK = 96, 512, 1848, 64
WIDE, CHUNKS = 256, 7
MAIN = WIDE * CHUNKS
LAST = FF - MAIN
CROSS = (1, 3, 5)
ALONG = (0, 2, 4, 6)


class Semaphores:
    def __init__(self):
        self.names = {}

    def of(self, *name):
        return self.names.setdefault(name, len(self.names))


def kernel(
    tok_in, gw, uw, gl_in, ul_in, gu_in, uu_in, out_s, inc_s,
    vg, vu, hid,
    tok, gl, ul, gu, uu, T, wg, wu, wc, wt, lc, l0, ls, lr, lf, uc, u0, us, ur, uq, ux, uf,
    part, parts_last, rx, qo, qa, ro, ra, acc, fs, fx, to, ta, tacc, ts, tx,
    ssem, rsem, lsem,
):
    row, col = lax.axis_index("row"), lax.axis_index("col")
    k, chip = row % 2, row // 2
    y, xm = row // 4, (row // 2) % 2
    xo = 1 - xm
    yp, yo, ym = (y + 1) % 4, (y + 2) % 4, (y + 3) % 4
    xh, z = col // 8, col % 8
    names = Semaphores()

    partner = (chip * 2 + 1 - k, col)
    cross = (y * 4 + xo * 2 + k, col)
    up_y = (yp * 4 + xm * 2 + k, col)
    down_y = (ym * 4 + xm * 2 + k, col)
    far_x = (row, (1 - xh) * 8 + z)
    far_partner = (chip * 2 + 1 - k, (1 - xh) * 8 + z)
    up_z = (row, xh * 8 + (z + 1) % 8)
    down_z = (row, xh * 8 + (z + 7) % 8)

    def ring_y(i):
        return ((y + i) % 4 * 4 + xm * 2 + k, col)

    def copy(src, dst, target, index):
        return pltpu.make_async_remote_copy(
            src_ref=src, dst_ref=dst, send_sem=ssem.at[index], recv_sem=rsem.at[index],
            device_id=target, device_id_type=MESH,
        )

    sent = []

    def send(src, dst, target, *name):
        c = copy(src, dst, target, names.of(*name))
        c.start()
        sent.append(c)
        return c

    barrier = pltpu.get_barrier_semaphore()
    pl.semaphore_signal(barrier, inc=1, device_id=partner, device_id_type=MESH)
    pl.semaphore_signal(barrier, inc=1, device_id=far_x, device_id_type=MESH)
    pl.semaphore_signal(barrier, inc=1, device_id=far_partner, device_id_type=MESH)
    pl.semaphore_signal(barrier, inc=1, device_id=cross, device_id_type=MESH)
    for i in range(1, 4):
        pl.semaphore_signal(barrier, inc=1, device_id=ring_y(i), device_id_type=MESH)
    for i in range(1, 8):
        pl.semaphore_signal(barrier, inc=1, device_id=(row, xh * 8 + (z + i) % 8), device_id_type=MESH)

    loads = [
        pltpu.make_async_copy(src, dst, lsem.at[2 + i])
        for i, (src, dst) in enumerate(((gu_in, gu), (uu_in, uu), (gl_in, gl), (ul_in, ul), (tok_in, tok)))
    ]
    for c in loads:
        c.start()
    load_g = pltpu.make_async_copy(gw, wg, lsem.at[0])
    load_u = pltpu.make_async_copy(uw, wu, lsem.at[1])
    load_g.start()
    load_u.start()

    for c in loads:
        c.wait()
    new, old = inc_s[0], out_s[0]
    for m, ref in enumerate((gu, uu)):
        b = ref[0]
        uc[m, 0:4] = jnp.where(new == row, b, jnp.zeros_like(b)).reshape(4, 16, FF)
        uc[m, 4:8] = jnp.where(old == row, -b, jnp.zeros_like(b)).reshape(4, 16, FF)
    for m, ref in enumerate((gl, ul)):
        a = ref[0]
        lc[8 * m:8 * m + 4] = jnp.where(new == col, a, jnp.zeros_like(a)).reshape(4, 16, DEPTH)
        lc[8 * m + 4:8 * m + 8] = jnp.where(old == col, a, jnp.zeros_like(a)).reshape(4, 16, DEPTH)
    pl.semaphore_wait(barrier, 14)

    even = k == z % 2
    odd = jnp.logical_not(even)
    xs, ys = (z // 2) % 2, col // 4
    t0 = [
        copy(tok.at[PART * p:PART * (p + 1)], T.at[xs, ys, PART * p:PART * (p + 1), DEPTH:], partner, names.of("t0", p))
        for p in range(PARTS)
    ]


    def far(p, half, place):
        rows = slice(PART * p, PART * (p + 1))
        dst = T.at[xs, place, rows, DEPTH * half:DEPTH * (half + 1)]
        return copy(tok.at[rows], dst, (far_x, far_partner)[half], names.of("h", p, half))

    @pl.when(odd)
    def _():
        for p in range(PARTS):
            t0[p].start()
        for p in range(PARTS):
            far(p, 1, ys).start()

    @pl.when(even)
    def _():
        for p in range(PARTS):
            far(p, 0, ys).start()
        T[xs, ys, :, 0:DEPTH] = tok[...]

    c_u0 = send(uc.at[1 - k], u0, partner, "u0")
    c_l0 = send(lc.at[pl.ds(8 * (1 - xh), 8)], l0, far_x, "l0")

    def block(zz, q, p):
        return T.at[(zz // 2) % 2, (xh + q) % 2 * 2 + zz // 4, PART * p:PART * (p + 1)]

    def hop(direction, stage, q, p, zz):
        target = (up_z, down_z)[direction]
        return copy(block(zz, q, p), block(zz, q, p), target, names.of("z", direction, stage, q, p))

    def source(direction, distance):
        return (z - distance + 8) % 8 if direction == 0 else (z + distance) % 8

    def forward(stage, q):
        for p in range(PARTS):
            for d in range(2):
                hop(d, stage, q, p, source(d, stage)).wait_recv()
                if stage < 3 or d == q:
                    hop(d, stage + 1, q, p, source(d, stage)).start()

    @pl.when(even)
    def _():
        for p in range(PARTS):
            t0[p].wait_recv()
            for d in range(2):
                hop(d, 1, 0, p, z).start()

    c_u0.wait_recv()
    us[...] = uc[k] + u0[...]
    u1 = [send(us.at[pl.ds((y + i) % 4 * 2, 2)], ur.at[i - 1], ring_y(i), "u1", i) for i in range(1, 4)]

    @pl.when(odd)
    def _():
        forward(1, 0)

    c_l0.wait_recv()
    ls[...] = lc[pl.ds(8 * xh, 8)] + l0[...]
    l1 = [send(ls.at[(z + i) % 8], lr.at[i - 1], (row, xh * 8 + (z + i) % 8), "l1", i) for i in range(1, 8)]

    @pl.when(even)
    def _():
        for p in range(PARTS):
            for half in range(2):
                far(p, half, (ys + 2) % 4).wait_recv()
            for d in range(2):
                hop(d, 1, 1, p, z).start()
        forward(2, 0)

    @pl.when(odd)
    def _():
        forward(1, 1)

    for c in u1:
        c.wait_recv()
    total = us[pl.ds(2 * y, 2)].astype(F32)
    for i in range(3):
        total = total + ur[i].astype(F32)
    uq[...] = total.astype(BF)
    c_ux = send(uq.at[xo], ux, cross, "ux")

    for c in l1:
        c.wait_recv()
    total = ls[z].astype(F32)
    for i in range(7):
        total = total + lr[i].astype(F32)
    mine = col
    lf[mine] = total.astype(BF)
    l2 = [send(lf.at[mine], lf.at[mine], (row, xh * 8 + (z + i) % 8), "l2", i) for i in range(1, 8)]
    l3 = [send(lf.at[mine], lf.at[mine], far_x, "l3", 0)]

    c_ux.wait_recv()
    uf[k, chip] = uq[xm] + ux[...]
    c_ua = send(uf.at[k, chip], uf.at[k, chip], cross, "ua")
    u2 = [send(uf.at[k, chip], uf.at[k, chip], ring_y(i), "u2", i) for i in range(1, 4)]
    u3 = [send(uf.at[k, chip], uf.at[k, chip], partner, "u3", 0)]

    @pl.when(odd)
    def _():
        forward(3, 0)

    beside = 2 * y + xo
    c_ua.wait_recv()
    u2b = [send(uf.at[k, beside], uf.at[k, beside], ring_y(i), "u2b", i) for i in range(1, 4)]
    u3.append(send(uf.at[k, beside], uf.at[k, beside], partner, "u3", 4))

    @pl.when(even)
    def _():
        forward(2, 1)

    for i in range(1, 8):
        l2[i - 1].wait_recv()
        s = xh * 8 + (z - i + 8) % 8
        l3.append(send(lf.at[s], lf.at[s], far_x, "l3", i))

    @pl.when(odd)
    def _():
        forward(3, 1)

    for i in range(1, 4):
        u2[i - 1].wait_recv()
        s = (y - i + 4) % 4 * 2 + xm
        u3.append(send(uf.at[k, s], uf.at[k, s], partner, "u3", i))
    for i in range(1, 4):
        u2b[i - 1].wait_recv()
        s = (y - i + 4) % 4 * 2 + xo
        u3.append(send(uf.at[k, s], uf.at[k, s], partner, "u3", 4 + i))

    for c in l3:
        c.wait_recv()
    for c in u3:
        c.wait_recv()
    load_g.wait()
    load_u.wait()

    def swap(j):
        return copy(wc.at[j, :, :, 0:DEPTH], wc.at[j, :, :, DEPTH:], partner, first_swap + j)

    for j in range(CHUNKS):
        index = names.of("w", j)
        if j == 0:
            first_swap = index

    def merged(w, m, cols):
        delta = lax.dot_general(
            uf[m, :, :, cols].reshape(2 * RANK, -1), lf[8 * m:8 * m + 8].reshape(2 * RANK, DEPTH),
            (((0,), (0,)), ((), ())), preferred_element_type=F32,
        )
        return (w[cols].astype(F32) + delta).astype(BF)

    def merge(j, carry):
        cols = pl.ds(pl.multiple_of(j * WIDE, WIDE), WIDE)
        for m, (w, v) in enumerate(((wg, vg), (wu, vu))):
            piece = merged(w, m, cols)
            v[cols] = piece
            wc[j, m, :, 0:DEPTH] = piece
        swap(j).start()
        return carry

    def merge_last():
        wt[:, 0:DEPTH] = jnp.zeros((128, DEPTH), BF)
        for m, (w, v) in enumerate(((wg, vg), (wu, vu))):
            piece = merged(w, m, slice(MAIN, FF))
            v[MAIN:FF] = piece
            wt[64 * m:64 * m + LAST, 0:DEPTH] = piece
        return send(wt.at[:, 0:DEPTH], wt.at[:, DEPTH:], partner, "wt")

    c_wt = merge_last()
    lax.fori_loop(0, AHEAD, merge, 0)

    @pl.when(even)
    def _():
        for p in range(PARTS):
            for d in range(2):
                hop(d, 4, d, p, source(d, 4)).wait_recv()

    def times(x, w):
        return lax.dot_general(
            T[x].reshape(4 * ROWS, 2 * DEPTH), w, (((1,), (1,)), ((), ())), preferred_element_type=F32
        )

    def compute(j, unit=None):
        swap(j).wait_recv()

        for m in range(2):
            def half(x, carry):
                part[j, m, x] = times(x, wc[j, m]).astype(BF).reshape(4, ROWS, WIDE)
                return carry

            lax.fori_loop(0, 2, half, 0)
            if unit is not None:
                unit.start(m)

    def compute_last(c_wt):
        c_wt.wait_recv()
        for x in range(2):
            p = times(x, wt[...])
            parts_last[x] = p.astype(BF).reshape(4, ROWS, 128)

    def add(ref, other):
        ref[...] = (ref[...].astype(F32) + other[...].astype(F32)).astype(BF)

    def finish(j, gate, up):
        h = gate / (1 + jnp.exp(-gate)) * up
        hid[:, j * WIDE:(j + 1) * WIDE] = h.astype(BF)

    ways = (up_y, down_y)
    near = (yp, ym)

    class Along:
        def __init__(self, i, j):
            self.i, self.j = i, j
            self.opposite, self.arrive, self.first = [], [], []

        def start(self, m):
            i, j = self.i, self.j
            self.opposite.append(send(part.at[j, m, :, yo], ro.at[i, m], ways[m], "ro", i, m))
            self.arrive.append(send(part.at[j, m, :, near[1 - m]], ra.at[i, 1 - m, m], ways[1 - m], "ra", i, 1 - m, m))

        def forward(self):
            i, j = self.i, self.j
            for d in range(2):
                self.opposite[d].wait_recv()
                add(part.at[j, d, :, near[d]], ro.at[i, d])
                self.arrive.append(send(part.at[j, d, :, near[d]], ra.at[i, d, d], ways[d], "ra", i, d, d))

        def gather(self):
            i, j = self.i, self.j
            for c in self.arrive:
                c.wait_recv()

            def total(m, x):
                return part[j, m, x, y].astype(F32) + ra[i, 0, m, x].astype(F32) + ra[i, 1, m, x].astype(F32)

            for m in range(2):
                fs[i, m] = total(m, xo).astype(BF)
            self.last = send(fs.at[i], fx.at[i], cross, "fx", i)
            for m in range(2):
                acc[i, m] = total(m, xm)

        def end(self):
            i, j = self.i, self.j
            self.last.wait_recv()
            finish(j, acc[i, 0] + fx[i, 0].astype(F32), acc[i, 1] + fx[i, 1].astype(F32))

    class Cross:
        def __init__(self, i, j):
            self.i, self.j = i, j
            self.opposite, self.arrive, self.first = [], [], []

        def start(self, m):
            i, j = self.i, self.j
            self.first.append(send(part.at[j, m, xo], rx.at[i, m], cross, "rx", i, m))

        def turn(self):
            i, j = self.i, self.j
            for m in range(2):
                self.first[m].wait_recv()
                add(part.at[j, m, xm], rx.at[i, m])
            self.opposite = [send(part.at[j, d, xm, yo], qo.at[i, d], ways[d], "qo", i, d) for d in range(2)]
            self.arrive = [send(part.at[j, 1 - d, xm, near[d]], qa.at[i, d, 1 - d], ways[d], "qa", i, d, 1 - d) for d in range(2)]

        def forward(self):
            i, j = self.i, self.j
            for d in range(2):
                self.opposite[d].wait_recv()
                add(part.at[j, d, xm, near[d]], qo.at[i, d])
                self.arrive.append(send(part.at[j, d, xm, near[d]], qa.at[i, d, d], ways[d], "qa", i, d, d))

        def end(self):
            i, j = self.i, self.j
            for c in self.arrive:
                c.wait_recv()

            def total(m):
                return part[j, m, xm, y].astype(F32) + qa[i, 0, m].astype(F32) + qa[i, 1, m].astype(F32)

            finish(j, total(0), total(1))

    class Last:
        def start(self):
            self.opposite = [send(parts_last.at[d, yo], to.at[d], ways[d], "to", d) for d in range(2)]
            self.arrive = [send(parts_last.at[1 - d, near[d]], ta.at[d, 1 - d], ways[d], "ta", d, 1 - d) for d in range(2)]

        def forward(self):
            for d in range(2):
                self.opposite[d].wait_recv()
                add(parts_last.at[d, near[d]], to.at[d])
                self.arrive.append(send(parts_last.at[d, near[d]], ta.at[d, d], ways[d], "ta", d, d))

        def gather(self):
            for c in self.arrive:
                c.wait_recv()

            def total(x):
                return parts_last[x, y].astype(F32) + ta[0, x].astype(F32) + ta[1, x].astype(F32)

            ts[...] = total(xo).astype(BF)
            self.last = send(ts, tx, cross, "tx")
            tacc[...] = total(xm)

        def end(self):
            self.last.wait_recv()
            gate = tacc[...] + tx[...].astype(F32)
            up = pltpu.roll(gate, 64, 1)
            h = gate / (1 + jnp.exp(-gate)) * up
            hid[:, MAIN:FF] = h[:, 0:LAST].astype(BF)

    along = [Along(i, j) for i, j in enumerate(ALONG)]
    crossed = [Cross(i, j) for i, j in enumerate(CROSS)]
    last = Last()
    compute_last(c_wt)
    last.start()
    for j in range(CHUNKS):
        compute(j, crossed[CROSS.index(j)] if j in CROSS else along[ALONG.index(j)])
        if j + AHEAD < CHUNKS:
            merge(j + AHEAD, 0)
    along[0].forward()
    along[1].forward()
    crossed[0].turn()
    along[2].forward()
    along[3].forward()
    last.forward()
    along[0].gather()
    crossed[0].forward()
    crossed[1].turn()
    along[1].gather()
    crossed[1].forward()
    along[2].gather()
    crossed[0].end()
    crossed[2].turn()
    along[3].gather()
    last.gather()
    crossed[2].forward()
    crossed[1].end()
    along[0].end()
    along[1].end()
    along[2].end()
    along[3].end()
    last.end()
    crossed[2].end()

    for c in sent:
        c.wait_send()
    for j in range(CHUNKS):
        swap(j).wait_send()

    @pl.when(even)
    def _():
        for p in range(PARTS):
            far(p, 0, ys).wait_send()
            for q in range(2):
                for d in range(2):
                    hop(d, 1, q, p, z).wait_send()
                    hop(d, 3, q, p, source(d, 2)).wait_send()

    @pl.when(odd)
    def _():
        for p in range(PARTS):
            t0[p].wait_send()
            far(p, 1, ys).wait_send()
            for q in range(2):
                for d in range(2):
                    hop(d, 2, q, p, source(d, 1)).wait_send()
                    if d == q:
                        hop(d, 4, q, p, source(d, 3)).wait_send()

    assert len(names.names) <= COPIES, len(names.names)


def store(a, b, c, x, y, z, sems):
    copies = [
        pltpu.make_async_copy(src, dst, sems.at[i]) for i, (src, dst) in enumerate(((a, x), (b, y), (c, z)))
    ]
    for c in copies:
        c.start()
    for c in copies:
        c.wait()


COPIES = 192
PARTS = 3
AHEAD = 2
PART = ROWS // PARTS


def body(tokens, gate_weight, up_weight, gate_lower, up_lower, *others):
    args = (
        tokens, gate_weight.T, up_weight.T, gate_lower.swapaxes(1, 2), up_lower.swapaxes(1, 2), *others
    )
    vmem = pl.BlockSpec(memory_space=pltpu.VMEM)
    smem = pl.BlockSpec(memory_space=pltpu.SMEM)
    anywhere = pl.BlockSpec(memory_space=pl.ANY)
    n_a, n_c = len(ALONG), len(CROSS)

    def b(*shape):
        return pltpu.VMEM(shape, BF)

    def f(*shape):
        return pltpu.VMEM(shape, F32)

    scratch = [
        b(ROWS, DEPTH), b(1, RANK, DEPTH), b(1, RANK, DEPTH), b(1, RANK, FF), b(1, RANK, FF),
        b(2, 4, ROWS, 2 * DEPTH),
        b(FF, DEPTH), b(FF, DEPTH),
        b(CHUNKS, 2, WIDE, 2 * DEPTH),
        b(128, 2 * DEPTH),
        b(16, 16, DEPTH), b(8, 16, DEPTH), b(8, 16, DEPTH), b(7, 16, DEPTH), b(16, 16, DEPTH),
        b(2, 8, 16, FF), b(8, 16, FF), b(8, 16, FF), b(3, 2, 16, FF), b(2, 16, FF), b(16, FF), b(2, 8, 16, FF),
        b(CHUNKS, 2, 2, 4, ROWS, WIDE),
        b(2, 4, ROWS, 128),
        b(n_c, 2, 4, ROWS, WIDE), b(n_c, 2, ROWS, WIDE), b(n_c, 2, 2, ROWS, WIDE),
        b(n_a, 2, 2, ROWS, WIDE), b(n_a, 2, 2, 2, ROWS, WIDE),
        f(n_a, 2, ROWS, WIDE), b(n_a, 2, ROWS, WIDE), b(n_a, 2, ROWS, WIDE),
        b(2, ROWS, 128), b(2, 2, ROWS, 128), f(ROWS, 128), b(ROWS, 128), b(ROWS, 128),
        pltpu.SemaphoreType.DMA((COPIES,)), pltpu.SemaphoreType.DMA((COPIES,)), pltpu.SemaphoreType.DMA((7,)),
    ]
    new_gate, new_up, hidden = pl.pallas_call(
        kernel,
        out_shape=(
            pltpu.VMEM((FF, DEPTH), BF),
            pltpu.VMEM((FF, DEPTH), BF),
            pltpu.VMEM((ROWS, FF), BF),
        ),
        in_specs=[anywhere] * 7 + [smem] * 2,
        out_specs=(vmem, vmem, vmem),
        scratch_shapes=scratch,
        compiler_params=pltpu.CompilerParams(
            collective_id=0, has_side_effects=True, vmem_limit_bytes=56 * 1024 * 1024
        ),
        cost_estimate=pl.CostEstimate(flops=7_000_000_000, bytes_accessed=10_000_000, transcendentals=200_000),
    )(*args)
    new_gate, new_up, hidden = pl.pallas_call(
        store,
        out_shape=(
            jax.ShapeDtypeStruct((FF, DEPTH), BF),
            jax.ShapeDtypeStruct((FF, DEPTH), BF),
            jax.ShapeDtypeStruct((ROWS, FF), BF),
        ),
        in_specs=[anywhere] * 3,
        out_specs=(anywhere,) * 3,
        scratch_shapes=[pltpu.SemaphoreType.DMA((3,))],
        compiler_params=pltpu.CompilerParams(vmem_limit_bytes=1024 * 1024),
    )(new_gate, new_up, hidden)
    return new_gate.T, new_up.T, hidden


def solution(mesh):
    return jax.shard_map(
        body,
        mesh=mesh,
        in_specs=(
            P("col", "row"),
            P("row", "col"),
            P("row", "col"),
            P("col", "row", None),
            P("col", "row", None),
            P("row", None, "col"),
            P("row", None, "col"),
            P(),
            P(),
        ),
        out_specs=(P("row", "col"), P("row", "col"), P("row", "col")),
        check_vma=False,
    )
```

```python
import jax
import jax.numpy as jnp
from jax import lax
from jax.experimental import pallas as pl
from jax.experimental.pallas import tpu as pltpu
from jax.sharding import PartitionSpec as P

MESH = pl.DeviceIdType.MESH
BF, F32 = jnp.bfloat16, jnp.float32
ROWS, DEPTH, FF, RANK = 96, 512, 1848, 64
WIDE, CHUNKS = 256, 7
MAIN = WIDE * CHUNKS
LAST = FF - MAIN
CROSS = (1, 3, 5)
ALONG = (0, 2, 4, 6)


class Semaphores:
    def __init__(self):
        self.names = {}

    def of(self, *name):
        return self.names.setdefault(name, len(self.names))


def kernel(
    tok_in, gw, uw, gl_in, ul_in, gu_in, uu_in, out_s, inc_s,
    vg, vu, hid,
    tok, gl, ul, gu, uu, T, wg, wu, wc, wt, lc, l0, ls, lr, lf, uc, u0, us, ur, uq, ux, uf,
    part, parts_last, rx, qo, qa, ro, ra, acc, fs, fx, to, ta, tacc, ts, tx,
    ssem, rsem, lsem,
):
    row, col = lax.axis_index("row"), lax.axis_index("col")
    k, chip = row % 2, row // 2
    y, xm = row // 4, (row // 2) % 2
    xo = 1 - xm
    yp, yo, ym = (y + 1) % 4, (y + 2) % 4, (y + 3) % 4
    xh, z = col // 8, col % 8
    names = Semaphores()

    partner = (chip * 2 + 1 - k, col)
    cross = (y * 4 + xo * 2 + k, col)
    up_y = (yp * 4 + xm * 2 + k, col)
    down_y = (ym * 4 + xm * 2 + k, col)
    far_x = (row, (1 - xh) * 8 + z)
    far_partner = (chip * 2 + 1 - k, (1 - xh) * 8 + z)
    up_z = (row, xh * 8 + (z + 1) % 8)
    down_z = (row, xh * 8 + (z + 7) % 8)

    def ring_y(i):
        return ((y + i) % 4 * 4 + xm * 2 + k, col)

    def copy(src, dst, target, index):
        return pltpu.make_async_remote_copy(
            src_ref=src, dst_ref=dst, send_sem=ssem.at[index], recv_sem=rsem.at[index],
            device_id=target, device_id_type=MESH,
        )

    sent = []

    def send(src, dst, target, *name):
        c = copy(src, dst, target, names.of(*name))
        c.start()
        sent.append(c)
        return c

    barrier = pltpu.get_barrier_semaphore()
    pl.semaphore_signal(barrier, inc=1, device_id=partner, device_id_type=MESH)
    pl.semaphore_signal(barrier, inc=1, device_id=far_x, device_id_type=MESH)
    pl.semaphore_signal(barrier, inc=1, device_id=far_partner, device_id_type=MESH)
    pl.semaphore_signal(barrier, inc=1, device_id=cross, device_id_type=MESH)
    for i in range(1, 4):
        pl.semaphore_signal(barrier, inc=1, device_id=ring_y(i), device_id_type=MESH)
    for i in range(1, 8):
        pl.semaphore_signal(barrier, inc=1, device_id=(row, xh * 8 + (z + i) % 8), device_id_type=MESH)

    loads = [
        pltpu.make_async_copy(src, dst, lsem.at[2 + i])
        for i, (src, dst) in enumerate(((gu_in, gu), (uu_in, uu), (gl_in, gl), (ul_in, ul), (tok_in, tok)))
    ]
    for c in loads:
        c.start()
    load_g = pltpu.make_async_copy(gw, wg, lsem.at[0])
    load_u = pltpu.make_async_copy(uw, wu, lsem.at[1])
    load_g.start()
    load_u.start()

    for c in loads:
        c.wait()
    new, old = inc_s[0], out_s[0]
    for m, ref in enumerate((gu, uu)):
        b = ref[0]
        uc[m, 0:4] = jnp.where(new == row, b, jnp.zeros_like(b)).reshape(4, 16, FF)
        uc[m, 4:8] = jnp.where(old == row, -b, jnp.zeros_like(b)).reshape(4, 16, FF)
    for m, ref in enumerate((gl, ul)):
        a = ref[0]
        lc[8 * m:8 * m + 4] = jnp.where(new == col, a, jnp.zeros_like(a)).reshape(4, 16, DEPTH)
        lc[8 * m + 4:8 * m + 8] = jnp.where(old == col, a, jnp.zeros_like(a)).reshape(4, 16, DEPTH)
    pl.semaphore_wait(barrier, 14)

    even = k == z % 2
    odd = jnp.logical_not(even)
    xs, ys = (z // 2) % 2, col // 4
    t0 = [
        copy(tok.at[PART * p:PART * (p + 1)], T.at[xs, ys, PART * p:PART * (p + 1), DEPTH:], partner, names.of("t0", p))
        for p in range(PARTS)
    ]


    def far(p, half, place):
        rows = slice(PART * p, PART * (p + 1))
        dst = T.at[xs, place, rows, DEPTH * half:DEPTH * (half + 1)]
        return copy(tok.at[rows], dst, (far_x, far_partner)[half], names.of("h", p, half))

    @pl.when(odd)
    def _():
        for p in range(PARTS):
            t0[p].start()
        for p in range(PARTS):
            far(p, 1, ys).start()

    @pl.when(even)
    def _():
        for p in range(PARTS):
            far(p, 0, ys).start()
        T[xs, ys, :, 0:DEPTH] = tok[...]

    c_u0 = send(uc.at[1 - k], u0, partner, "u0")
    c_l0 = send(lc.at[pl.ds(8 * (1 - xh), 8)], l0, far_x, "l0")

    def block(zz, q, p):
        return T.at[(zz // 2) % 2, (xh + q) % 2 * 2 + zz // 4, PART * p:PART * (p + 1)]

    def hop(direction, stage, q, p, zz):
        target = (up_z, down_z)[direction]
        return copy(block(zz, q, p), block(zz, q, p), target, names.of("z", direction, stage, q, p))

    def source(direction, distance):
        return (z - distance + 8) % 8 if direction == 0 else (z + distance) % 8

    def forward(stage, q):
        for p in range(PARTS):
            for d in range(2):
                hop(d, stage, q, p, source(d, stage)).wait_recv()
                if stage < 3 or d == q:
                    hop(d, stage + 1, q, p, source(d, stage)).start()

    @pl.when(even)
    def _():
        for p in range(PARTS):
            t0[p].wait_recv()
            for d in range(2):
                hop(d, 1, 0, p, z).start()

    c_u0.wait_recv()
    us[...] = uc[k] + u0[...]
    u1 = [send(us.at[pl.ds((y + i) % 4 * 2, 2)], ur.at[i - 1], ring_y(i), "u1", i) for i in range(1, 4)]

    @pl.when(odd)
    def _():
        forward(1, 0)

    c_l0.wait_recv()
    ls[...] = lc[pl.ds(8 * xh, 8)] + l0[...]
    l1 = [send(ls.at[(z + i) % 8], lr.at[i - 1], (row, xh * 8 + (z + i) % 8), "l1", i) for i in range(1, 8)]

    @pl.when(even)
    def _():
        for p in range(PARTS):
            for half in range(2):
                far(p, half, (ys + 2) % 4).wait_recv()
            for d in range(2):
                hop(d, 1, 1, p, z).start()
        forward(2, 0)

    @pl.when(odd)
    def _():
        forward(1, 1)

    for c in u1:
        c.wait_recv()
    total = us[pl.ds(2 * y, 2)].astype(F32)
    for i in range(3):
        total = total + ur[i].astype(F32)
    uq[...] = total.astype(BF)
    c_ux = send(uq.at[xo], ux, cross, "ux")

    for c in l1:
        c.wait_recv()
    total = ls[z].astype(F32)
    for i in range(7):
        total = total + lr[i].astype(F32)
    mine = col
    lf[mine] = total.astype(BF)
    l2 = [send(lf.at[mine], lf.at[mine], (row, xh * 8 + (z + i) % 8), "l2", i) for i in range(1, 8)]
    l3 = [send(lf.at[mine], lf.at[mine], far_x, "l3", 0)]

    c_ux.wait_recv()
    uf[k, chip] = uq[xm] + ux[...]
    c_ua = send(uf.at[k, chip], uf.at[k, chip], cross, "ua")
    u2 = [send(uf.at[k, chip], uf.at[k, chip], ring_y(i), "u2", i) for i in range(1, 4)]
    u3 = [send(uf.at[k, chip], uf.at[k, chip], partner, "u3", 0)]

    @pl.when(odd)
    def _():
        forward(3, 0)

    beside = 2 * y + xo
    c_ua.wait_recv()
    u2b = [send(uf.at[k, beside], uf.at[k, beside], ring_y(i), "u2b", i) for i in range(1, 4)]
    u3.append(send(uf.at[k, beside], uf.at[k, beside], partner, "u3", 4))

    @pl.when(even)
    def _():
        forward(2, 1)

    for i in range(1, 8):
        l2[i - 1].wait_recv()
        s = xh * 8 + (z - i + 8) % 8
        l3.append(send(lf.at[s], lf.at[s], far_x, "l3", i))

    @pl.when(odd)
    def _():
        forward(3, 1)

    for i in range(1, 4):
        u2[i - 1].wait_recv()
        s = (y - i + 4) % 4 * 2 + xm
        u3.append(send(uf.at[k, s], uf.at[k, s], partner, "u3", i))
    for i in range(1, 4):
        u2b[i - 1].wait_recv()
        s = (y - i + 4) % 4 * 2 + xo
        u3.append(send(uf.at[k, s], uf.at[k, s], partner, "u3", 4 + i))

    for c in l3:
        c.wait_recv()
    for c in u3:
        c.wait_recv()
    load_g.wait()
    load_u.wait()

    def swap(j):
        return copy(wc.at[j, :, :, 0:DEPTH], wc.at[j, :, :, DEPTH:], partner, first_swap + j)

    for j in range(CHUNKS):
        index = names.of("w", j)
        if j == 0:
            first_swap = index

    def merged(w, m, cols):
        delta = lax.dot_general(
            uf[m, :, :, cols].reshape(2 * RANK, -1), lf[8 * m:8 * m + 8].reshape(2 * RANK, DEPTH),
            (((0,), (0,)), ((), ())), preferred_element_type=F32,
        )
        return (w[cols].astype(F32) + delta).astype(BF)

    def merge(j, carry):
        cols = pl.ds(pl.multiple_of(j * WIDE, WIDE), WIDE)
        for m, (w, v) in enumerate(((wg, vg), (wu, vu))):
            piece = merged(w, m, cols)
            v[cols] = piece
            wc[j, m, :, 0:DEPTH] = piece
        swap(j).start()
        return carry

    def merge_last():
        wt[:, 0:DEPTH] = jnp.zeros((128, DEPTH), BF)
        for m, (w, v) in enumerate(((wg, vg), (wu, vu))):
            piece = merged(w, m, slice(MAIN, FF))
            v[MAIN:FF] = piece
            wt[64 * m:64 * m + LAST, 0:DEPTH] = piece
        return send(wt.at[:, 0:DEPTH], wt.at[:, DEPTH:], partner, "wt")

    c_wt = merge_last()
    merge(0, 0)

    @pl.when(even)
    def _():
        for p in range(PARTS):
            for d in range(2):
                hop(d, 4, d, p, source(d, 4)).wait_recv()

    def times(x, w):
        return lax.dot_general(
            T[x].reshape(4 * ROWS, 2 * DEPTH), w, (((1,), (1,)), ((), ())), preferred_element_type=F32
        )

    def compute(j, unit=None):
        swap(j).wait_recv()

        for m in range(2):
            def half(x, carry):
                part[j, m, x] = times(x, wc[j, m]).astype(BF).reshape(4, ROWS, WIDE)
                return carry

            lax.fori_loop(0, 2, half, 0)
            if unit is not None:
                unit.start(m)

    def compute_last(c_wt):
        c_wt.wait_recv()
        for x in range(2):
            p = times(x, wt[...])
            parts_last[x] = p.astype(BF).reshape(4, ROWS, 128)

    def add(ref, other):
        ref[...] = (ref[...].astype(F32) + other[...].astype(F32)).astype(BF)

    def finish(j, gate, up):
        h = gate / (1 + jnp.exp(-gate)) * up
        hid[:, j * WIDE:(j + 1) * WIDE] = h.astype(BF)

    ways = (up_y, down_y)
    near = (yp, ym)

    class Along:
        def __init__(self, i, j):
            self.i, self.j = i, j
            self.opposite, self.arrive, self.first = [], [], []

        def start(self, m):
            i, j = self.i, self.j
            self.opposite.append(send(part.at[j, m, :, yo], ro.at[i, m], ways[m], "ro", i, m))
            self.arrive.append(send(part.at[j, m, :, near[1 - m]], ra.at[i, 1 - m, m], ways[1 - m], "ra", i, 1 - m, m))

        def forward(self):
            i, j = self.i, self.j
            for d in range(2):
                self.opposite[d].wait_recv()
                add(part.at[j, d, :, near[d]], ro.at[i, d])
                self.arrive.append(send(part.at[j, d, :, near[d]], ra.at[i, d, d], ways[d], "ra", i, d, d))

        def gather(self):
            i, j = self.i, self.j
            for c in self.arrive:
                c.wait_recv()

            def total(m, x):
                return part[j, m, x, y].astype(F32) + ra[i, 0, m, x].astype(F32) + ra[i, 1, m, x].astype(F32)

            for m in range(2):
                fs[i, m] = total(m, xo).astype(BF)
            self.last = send(fs.at[i], fx.at[i], cross, "fx", i)
            for m in range(2):
                acc[i, m] = total(m, xm)

        def end(self):
            i, j = self.i, self.j
            self.last.wait_recv()
            finish(j, acc[i, 0] + fx[i, 0].astype(F32), acc[i, 1] + fx[i, 1].astype(F32))

    class Cross:
        def __init__(self, i, j):
            self.i, self.j = i, j
            self.opposite, self.arrive, self.first = [], [], []

        def start(self, m):
            i, j = self.i, self.j
            self.first.append(send(part.at[j, m, xo], rx.at[i, m], cross, "rx", i, m))

        def turn(self):
            i, j = self.i, self.j
            for m in range(2):
                self.first[m].wait_recv()
                add(part.at[j, m, xm], rx.at[i, m])
            self.opposite = [send(part.at[j, d, xm, yo], qo.at[i, d], ways[d], "qo", i, d) for d in range(2)]
            self.arrive = [send(part.at[j, 1 - d, xm, near[d]], qa.at[i, d, 1 - d], ways[d], "qa", i, d, 1 - d) for d in range(2)]

        def forward(self):
            i, j = self.i, self.j
            for d in range(2):
                self.opposite[d].wait_recv()
                add(part.at[j, d, xm, near[d]], qo.at[i, d])
                self.arrive.append(send(part.at[j, d, xm, near[d]], qa.at[i, d, d], ways[d], "qa", i, d, d))

        def end(self):
            i, j = self.i, self.j
            for c in self.arrive:
                c.wait_recv()

            def total(m):
                return part[j, m, xm, y].astype(F32) + qa[i, 0, m].astype(F32) + qa[i, 1, m].astype(F32)

            finish(j, total(0), total(1))

    class Last:
        def start(self):
            self.opposite = [send(parts_last.at[d, yo], to.at[d], ways[d], "to", d) for d in range(2)]
            self.arrive = [send(parts_last.at[1 - d, near[d]], ta.at[d, 1 - d], ways[d], "ta", d, 1 - d) for d in range(2)]

        def forward(self):
            for d in range(2):
                self.opposite[d].wait_recv()
                add(parts_last.at[d, near[d]], to.at[d])
                self.arrive.append(send(parts_last.at[d, near[d]], ta.at[d, d], ways[d], "ta", d, d))

        def gather(self):
            for c in self.arrive:
                c.wait_recv()

            def total(x):
                return parts_last[x, y].astype(F32) + ta[0, x].astype(F32) + ta[1, x].astype(F32)

            ts[...] = total(xo).astype(BF)
            self.last = send(ts, tx, cross, "tx")
            tacc[...] = total(xm)

        def end(self):
            self.last.wait_recv()
            gate = tacc[...] + tx[...].astype(F32)
            up = pltpu.roll(gate, 64, 1)
            h = gate / (1 + jnp.exp(-gate)) * up
            hid[:, MAIN:FF] = h[:, 0:LAST].astype(BF)

    along = [Along(i, j) for i, j in enumerate(ALONG)]
    crossed = [Cross(i, j) for i, j in enumerate(CROSS)]
    last = Last()
    waited = len(sent)
    compute_last(c_wt)
    last.start()
    for j in range(1, AHEAD):
        merge(j, 0)
    for j in range(CHUNKS):
        compute(j, crossed[CROSS.index(j)] if j in CROSS else along[ALONG.index(j)])
        if j + AHEAD < CHUNKS:
            merge(j + AHEAD, 0)
    along[0].forward()
    along[1].forward()
    crossed[0].turn()
    along[2].forward()
    along[3].forward()
    last.forward()
    along[0].gather()
    crossed[0].forward()
    crossed[1].turn()
    along[1].gather()
    crossed[1].forward()
    along[2].gather()
    crossed[0].end()
    for c in sent[:waited]:
        c.wait_send()
    for j in range(CHUNKS):
        swap(j).wait_send()

    @pl.when(even)
    def _():
        for p in range(PARTS):
            far(p, 0, ys).wait_send()
            for q in range(2):
                for d in range(2):
                    hop(d, 1, q, p, z).wait_send()
                    hop(d, 3, q, p, source(d, 2)).wait_send()

    @pl.when(odd)
    def _():
        for p in range(PARTS):
            t0[p].wait_send()
            far(p, 1, ys).wait_send()
            for q in range(2):
                for d in range(2):
                    hop(d, 2, q, p, source(d, 1)).wait_send()
                    if d == q:
                        hop(d, 4, q, p, source(d, 3)).wait_send()

    crossed[2].turn()
    along[3].gather()
    last.gather()
    crossed[2].forward()
    crossed[1].end()
    along[0].end()
    along[1].end()
    along[2].end()
    along[3].end()
    last.end()
    crossed[2].end()

    for c in sent[waited:]:
        c.wait_send()
    assert len(names.names) <= COPIES, len(names.names)


def store(a, b, c, x, y, z, sems):
    copies = [
        pltpu.make_async_copy(src, dst, sems.at[i]) for i, (src, dst) in enumerate(((a, x), (b, y), (c, z)))
    ]
    for c in copies:
        c.start()
    for c in copies:
        c.wait()


COPIES = 192
PARTS = 3
AHEAD = 2
PART = ROWS // PARTS


def body(tokens, gate_weight, up_weight, gate_lower, up_lower, *others):
    args = (
        tokens, gate_weight.T, up_weight.T, gate_lower.swapaxes(1, 2), up_lower.swapaxes(1, 2), *others
    )
    vmem = pl.BlockSpec(memory_space=pltpu.VMEM)
    smem = pl.BlockSpec(memory_space=pltpu.SMEM)
    anywhere = pl.BlockSpec(memory_space=pl.ANY)
    n_a, n_c = len(ALONG), len(CROSS)

    def b(*shape):
        return pltpu.VMEM(shape, BF)

    def f(*shape):
        return pltpu.VMEM(shape, F32)

    scratch = [
        b(ROWS, DEPTH), b(1, RANK, DEPTH), b(1, RANK, DEPTH), b(1, RANK, FF), b(1, RANK, FF),
        b(2, 4, ROWS, 2 * DEPTH),
        b(FF, DEPTH), b(FF, DEPTH),
        b(CHUNKS, 2, WIDE, 2 * DEPTH),
        b(128, 2 * DEPTH),
        b(16, 16, DEPTH), b(8, 16, DEPTH), b(8, 16, DEPTH), b(7, 16, DEPTH), b(16, 16, DEPTH),
        b(2, 8, 16, FF), b(8, 16, FF), b(8, 16, FF), b(3, 2, 16, FF), b(2, 16, FF), b(16, FF), b(2, 8, 16, FF),
        b(CHUNKS, 2, 2, 4, ROWS, WIDE),
        b(2, 4, ROWS, 128),
        b(n_c, 2, 4, ROWS, WIDE), b(n_c, 2, ROWS, WIDE), b(n_c, 2, 2, ROWS, WIDE),
        b(n_a, 2, 2, ROWS, WIDE), b(n_a, 2, 2, 2, ROWS, WIDE),
        f(n_a, 2, ROWS, WIDE), b(n_a, 2, ROWS, WIDE), b(n_a, 2, ROWS, WIDE),
        b(2, ROWS, 128), b(2, 2, ROWS, 128), f(ROWS, 128), b(ROWS, 128), b(ROWS, 128),
        pltpu.SemaphoreType.DMA((COPIES,)), pltpu.SemaphoreType.DMA((COPIES,)), pltpu.SemaphoreType.DMA((7,)),
    ]
    new_gate, new_up, hidden = pl.pallas_call(
        kernel,
        out_shape=(
            pltpu.VMEM((FF, DEPTH), BF),
            pltpu.VMEM((FF, DEPTH), BF),
            pltpu.VMEM((ROWS, FF), BF),
        ),
        in_specs=[anywhere] * 7 + [smem] * 2,
        out_specs=(vmem, vmem, vmem),
        scratch_shapes=scratch,
        compiler_params=pltpu.CompilerParams(
            collective_id=0, has_side_effects=True, vmem_limit_bytes=56 * 1024 * 1024
        ),
        cost_estimate=pl.CostEstimate(flops=7_000_000_000, bytes_accessed=10_000_000, transcendentals=200_000),
    )(*args)
    new_gate, new_up, hidden = pl.pallas_call(
        store,
        out_shape=(
            jax.ShapeDtypeStruct((FF, DEPTH), BF),
            jax.ShapeDtypeStruct((FF, DEPTH), BF),
            jax.ShapeDtypeStruct((ROWS, FF), BF),
        ),
        in_specs=[anywhere] * 3,
        out_specs=(anywhere,) * 3,
        scratch_shapes=[pltpu.SemaphoreType.DMA((3,))],
        compiler_params=pltpu.CompilerParams(vmem_limit_bytes=1024 * 1024),
    )(new_gate, new_up, hidden)
    return new_gate.T, new_up.T, hidden


def solution(mesh):
    return jax.shard_map(
        body,
        mesh=mesh,
        in_specs=(
            P("col", "row"),
            P("row", "col"),
            P("row", "col"),
            P("col", "row", None),
            P("col", "row", None),
            P("row", None, "col"),
            P("row", None, "col"),
            P(),
            P(),
        ),
        out_specs=(P("row", "col"), P("row", "col"), P("row", "col")),
        check_vma=False,
    )
```

```python
import jax
import jax.numpy as jnp
from jax import lax
from jax.experimental import pallas as pl
from jax.experimental.pallas import tpu as pltpu
from jax.sharding import PartitionSpec as P

MESH = pl.DeviceIdType.MESH
BF, F32 = jnp.bfloat16, jnp.float32
ROWS, DEPTH, FF, RANK = 96, 512, 1848, 64
WIDE, CHUNKS = 256, 7
MAIN = WIDE * CHUNKS
LAST = FF - MAIN
CROSS = (1, 3, 5)
ALONG = (0, 2, 4, 6)


class Semaphores:
    def __init__(self):
        self.names = {}

    def of(self, *name):
        return self.names.setdefault(name, len(self.names))


def kernel(
    tok_in, gw, uw, gl_in, ul_in, gu_in, uu_in, out_s, inc_s,
    vg, vu, hid,
    tok, gl, ul, gu, uu, T, wg, wu, wc, wt, lc, l0, ls, lr, lf, uc, u0, us, ur, uq, ux, uf,
    part, parts_last, rx, qo, qa, ro, ra, acc, fs, fx, to, ta, tacc, ts, tx,
    ssem, rsem, lsem,
):
    row, col = lax.axis_index("row"), lax.axis_index("col")
    k, chip = row % 2, row // 2
    y, xm = row // 4, (row // 2) % 2
    xo = 1 - xm
    yp, yo, ym = (y + 1) % 4, (y + 2) % 4, (y + 3) % 4
    xh, z = col // 8, col % 8
    names = Semaphores()

    partner = (chip * 2 + 1 - k, col)
    cross = (y * 4 + xo * 2 + k, col)
    up_y = (yp * 4 + xm * 2 + k, col)
    down_y = (ym * 4 + xm * 2 + k, col)
    far_x = (row, (1 - xh) * 8 + z)
    far_partner = (chip * 2 + 1 - k, (1 - xh) * 8 + z)
    up_z = (row, xh * 8 + (z + 1) % 8)
    down_z = (row, xh * 8 + (z + 7) % 8)

    def ring_y(i):
        return ((y + i) % 4 * 4 + xm * 2 + k, col)

    def copy(src, dst, target, index):
        return pltpu.make_async_remote_copy(
            src_ref=src, dst_ref=dst, send_sem=ssem.at[index], recv_sem=rsem.at[index],
            device_id=target, device_id_type=MESH,
        )

    sent = []

    def send(src, dst, target, *name):
        c = copy(src, dst, target, names.of(*name))
        c.start()
        sent.append(c)
        return c

    barrier = pltpu.get_barrier_semaphore()
    pl.semaphore_signal(barrier, inc=1, device_id=partner, device_id_type=MESH)
    pl.semaphore_signal(barrier, inc=1, device_id=far_x, device_id_type=MESH)
    pl.semaphore_signal(barrier, inc=1, device_id=far_partner, device_id_type=MESH)
    pl.semaphore_signal(barrier, inc=1, device_id=cross, device_id_type=MESH)
    for i in range(1, 4):
        pl.semaphore_signal(barrier, inc=1, device_id=ring_y(i), device_id_type=MESH)
    for i in range(1, 8):
        pl.semaphore_signal(barrier, inc=1, device_id=(row, xh * 8 + (z + i) % 8), device_id_type=MESH)

    loads = [
        pltpu.make_async_copy(src, dst, lsem.at[2 + i])
        for i, (src, dst) in enumerate(((gu_in, gu), (uu_in, uu), (gl_in, gl), (ul_in, ul), (tok_in, tok)))
    ]
    for c in loads:
        c.start()
    load_g = pltpu.make_async_copy(gw, wg, lsem.at[0])
    load_u = pltpu.make_async_copy(uw, wu, lsem.at[1])
    load_g.start()
    load_u.start()

    for c in loads:
        c.wait()
    new, old = inc_s[0], out_s[0]
    for m, ref in enumerate((gu, uu)):
        b = ref[0]
        uc[m, 0:4] = jnp.where(new == row, b, jnp.zeros_like(b)).reshape(4, 16, FF)
        uc[m, 4:8] = jnp.where(old == row, -b, jnp.zeros_like(b)).reshape(4, 16, FF)
    for m, ref in enumerate((gl, ul)):
        a = ref[0]
        lc[8 * m:8 * m + 4] = jnp.where(new == col, a, jnp.zeros_like(a)).reshape(4, 16, DEPTH)
        lc[8 * m + 4:8 * m + 8] = jnp.where(old == col, a, jnp.zeros_like(a)).reshape(4, 16, DEPTH)
    pl.semaphore_wait(barrier, 14)

    even = k == z % 2
    odd = jnp.logical_not(even)
    xs, ys = (z // 2) % 2, col // 4
    t0 = [
        copy(tok.at[PART * p:PART * (p + 1)], T.at[xs, ys, PART * p:PART * (p + 1), DEPTH:], partner, names.of("t0", p))
        for p in range(PARTS)
    ]


    def far(p, half, place):
        rows = slice(PART * p, PART * (p + 1))
        dst = T.at[xs, place, rows, DEPTH * half:DEPTH * (half + 1)]
        return copy(tok.at[rows], dst, (far_x, far_partner)[half], names.of("h", p, half))

    @pl.when(odd)
    def _():
        for p in range(PARTS):
            t0[p].start()
        for p in range(PARTS):
            far(p, 1, ys).start()

    @pl.when(even)
    def _():
        for p in range(PARTS):
            far(p, 0, ys).start()
        T[xs, ys, :, 0:DEPTH] = tok[...]

    c_u0 = send(uc.at[1 - k], u0, partner, "u0")
    c_l0 = send(lc.at[pl.ds(8 * (1 - xh), 8)], l0, far_x, "l0")

    def block(zz, q, p):
        return T.at[(zz // 2) % 2, (xh + q) % 2 * 2 + zz // 4, PART * p:PART * (p + 1)]

    def hop(direction, stage, q, p, zz):
        target = (up_z, down_z)[direction]
        return copy(block(zz, q, p), block(zz, q, p), target, names.of("z", direction, stage, q, p))

    def source(direction, distance):
        return (z - distance + 8) % 8 if direction == 0 else (z + distance) % 8

    def forward(stage, q):
        for p in range(PARTS):
            for d in range(2):
                hop(d, stage, q, p, source(d, stage)).wait_recv()
                if stage < 3 or d == q:
                    hop(d, stage + 1, q, p, source(d, stage)).start()

    @pl.when(even)
    def _():
        for p in range(PARTS):
            t0[p].wait_recv()
            for d in range(2):
                hop(d, 1, 0, p, z).start()

    c_u0.wait_recv()
    us[...] = uc[k] + u0[...]
    u1 = [send(us.at[pl.ds((y + i) % 4 * 2, 2)], ur.at[i - 1], ring_y(i), "u1", i) for i in range(1, 4)]

    @pl.when(odd)
    def _():
        forward(1, 0)

    c_l0.wait_recv()
    ls[...] = lc[pl.ds(8 * xh, 8)] + l0[...]
    l1 = [send(ls.at[(z + i) % 8], lr.at[i - 1], (row, xh * 8 + (z + i) % 8), "l1", i) for i in range(1, 8)]

    @pl.when(even)
    def _():
        for p in range(PARTS):
            for half in range(2):
                far(p, half, (ys + 2) % 4).wait_recv()
            for d in range(2):
                hop(d, 1, 1, p, z).start()
        forward(2, 0)

    @pl.when(odd)
    def _():
        forward(1, 1)

    for c in u1:
        c.wait_recv()
    total = us[pl.ds(2 * y, 2)].astype(F32)
    for i in range(3):
        total = total + ur[i].astype(F32)
    uq[...] = total.astype(BF)
    c_ux = send(uq.at[xo], ux, cross, "ux")

    for c in l1:
        c.wait_recv()
    total = ls[z].astype(F32)
    for i in range(7):
        total = total + lr[i].astype(F32)
    mine = col
    lf[mine] = total.astype(BF)
    l2 = [send(lf.at[mine], lf.at[mine], (row, xh * 8 + (z + i) % 8), "l2", i) for i in range(1, 8)]
    l3 = [send(lf.at[mine], lf.at[mine], far_x, "l3", 0)]

    c_ux.wait_recv()
    uf[k, chip] = uq[xm] + ux[...]
    c_ua = send(uf.at[k, chip], uf.at[k, chip], cross, "ua")
    u2 = [send(uf.at[k, chip], uf.at[k, chip], ring_y(i), "u2", i) for i in range(1, 4)]
    u3 = [send(uf.at[k, chip], uf.at[k, chip], partner, "u3", 0)]

    @pl.when(odd)
    def _():
        forward(3, 0)

    beside = 2 * y + xo
    c_ua.wait_recv()
    u2b = [send(uf.at[k, beside], uf.at[k, beside], ring_y(i), "u2b", i) for i in range(1, 4)]
    u3.append(send(uf.at[k, beside], uf.at[k, beside], partner, "u3", 4))

    @pl.when(even)
    def _():
        forward(2, 1)

    for i in range(1, 8):
        l2[i - 1].wait_recv()
        s = xh * 8 + (z - i + 8) % 8
        l3.append(send(lf.at[s], lf.at[s], far_x, "l3", i))

    @pl.when(odd)
    def _():
        forward(3, 1)

    for i in range(1, 4):
        u2[i - 1].wait_recv()
        s = (y - i + 4) % 4 * 2 + xm
        u3.append(send(uf.at[k, s], uf.at[k, s], partner, "u3", i))
    for i in range(1, 4):
        u2b[i - 1].wait_recv()
        s = (y - i + 4) % 4 * 2 + xo
        u3.append(send(uf.at[k, s], uf.at[k, s], partner, "u3", 4 + i))

    for c in l3:
        c.wait_recv()
    for c in u3:
        c.wait_recv()
    load_g.wait()
    load_u.wait()

    def swap(j):
        return copy(wc.at[j, :, :, 0:DEPTH], wc.at[j, :, :, DEPTH:], partner, first_swap + j)

    for j in range(CHUNKS):
        index = names.of("w", j)
        if j == 0:
            first_swap = index

    def merged(w, m, cols):
        delta = lax.dot_general(
            uf[m, :, :, cols].reshape(2 * RANK, -1), lf[8 * m:8 * m + 8].reshape(2 * RANK, DEPTH),
            (((0,), (0,)), ((), ())), preferred_element_type=F32,
        )
        return (w[cols].astype(F32) + delta).astype(BF)

    def merge(j, carry):
        cols = pl.ds(pl.multiple_of(j * WIDE, WIDE), WIDE)
        for m, (w, v) in enumerate(((wg, vg), (wu, vu))):
            piece = merged(w, m, cols)
            v[cols] = piece
            wc[j, m, :, 0:DEPTH] = piece
        swap(j).start()
        return carry

    def merge_last():
        wt[:, 0:DEPTH] = jnp.zeros((128, DEPTH), BF)
        for m, (w, v) in enumerate(((wg, vg), (wu, vu))):
            piece = merged(w, m, slice(MAIN, FF))
            v[MAIN:FF] = piece
            wt[64 * m:64 * m + LAST, 0:DEPTH] = piece
        return send(wt.at[:, 0:DEPTH], wt.at[:, DEPTH:], partner, "wt")

    c_wt = merge_last()
    merge(0, 0)

    @pl.when(even)
    def _():
        for p in range(PARTS):
            for d in range(2):
                hop(d, 4, d, p, source(d, 4)).wait_recv()

    def times(x, w):
        return lax.dot_general(
            T[x].reshape(4 * ROWS, 2 * DEPTH), w, (((1,), (1,)), ((), ())), preferred_element_type=F32
        )

    def compute(j, unit=None):
        swap(j).wait_recv()

        for m in range(2):
            def half(x, carry):
                part[j, m, x] = times(x, wc[j, m]).astype(BF).reshape(4, ROWS, WIDE)
                return carry

            lax.fori_loop(0, 2, half, 0)
            if unit is not None:
                unit.start(m)

    def compute_last(c_wt):
        c_wt.wait_recv()
        for x in range(2):
            p = times(x, wt[...])
            parts_last[x] = p.astype(BF).reshape(4, ROWS, 128)

    def add(ref, other):
        ref[...] = (ref[...].astype(F32) + other[...].astype(F32)).astype(BF)

    def finish(j, gate, up):
        h = gate / (1 + jnp.exp(-gate)) * up
        hid[:, j * WIDE:(j + 1) * WIDE] = h.astype(BF)

    ways = (up_y, down_y)
    near = (yp, ym)

    class Along:
        def __init__(self, i, j):
            self.i, self.j = i, j
            self.opposite, self.arrive, self.first = [], [], []

        def start(self, m):
            i, j = self.i, self.j
            self.opposite.append(send(part.at[j, m, :, yo], ro.at[i, m], ways[m], "ro", i, m))
            self.arrive.append(send(part.at[j, m, :, near[1 - m]], ra.at[i, 1 - m, m], ways[1 - m], "ra", i, 1 - m, m))

        def forward(self):
            i, j = self.i, self.j
            for d in range(2):
                self.opposite[d].wait_recv()
                add(part.at[j, d, :, near[d]], ro.at[i, d])
                self.arrive.append(send(part.at[j, d, :, near[d]], ra.at[i, d, d], ways[d], "ra", i, d, d))

        def gather(self):
            i, j = self.i, self.j
            for c in self.arrive:
                c.wait_recv()

            def total(m, x):
                return part[j, m, x, y].astype(F32) + ra[i, 0, m, x].astype(F32) + ra[i, 1, m, x].astype(F32)

            for m in range(2):
                fs[i, m] = total(m, xo).astype(BF)
            self.last = send(fs.at[i], fx.at[i], cross, "fx", i)
            for m in range(2):
                acc[i, m] = total(m, xm)

        def end(self):
            i, j = self.i, self.j
            self.last.wait_recv()
            finish(j, acc[i, 0] + fx[i, 0].astype(F32), acc[i, 1] + fx[i, 1].astype(F32))

    class Cross:
        def __init__(self, i, j):
            self.i, self.j = i, j
            self.opposite, self.arrive, self.first = [], [], []

        def start(self, m):
            i, j = self.i, self.j
            self.first.append(send(part.at[j, m, xo], rx.at[i, m], cross, "rx", i, m))

        def turn(self):
            i, j = self.i, self.j
            for m in range(2):
                self.first[m].wait_recv()
                add(part.at[j, m, xm], rx.at[i, m])
            self.opposite = [send(part.at[j, d, xm, yo], qo.at[i, d], ways[d], "qo", i, d) for d in range(2)]
            self.arrive = [send(part.at[j, 1 - d, xm, near[d]], qa.at[i, d, 1 - d], ways[d], "qa", i, d, 1 - d) for d in range(2)]

        def forward(self):
            i, j = self.i, self.j
            for d in range(2):
                self.opposite[d].wait_recv()
                add(part.at[j, d, xm, near[d]], qo.at[i, d])
                self.arrive.append(send(part.at[j, d, xm, near[d]], qa.at[i, d, d], ways[d], "qa", i, d, d))

        def end(self):
            i, j = self.i, self.j
            for c in self.arrive:
                c.wait_recv()

            def total(m):
                return part[j, m, xm, y].astype(F32) + qa[i, 0, m].astype(F32) + qa[i, 1, m].astype(F32)

            finish(j, total(0), total(1))

    class Last:
        def start(self):
            self.opposite = [send(parts_last.at[d, yo], to.at[d], ways[d], "to", d) for d in range(2)]
            self.arrive = [send(parts_last.at[1 - d, near[d]], ta.at[d, 1 - d], ways[d], "ta", d, 1 - d) for d in range(2)]

        def forward(self):
            for d in range(2):
                self.opposite[d].wait_recv()
                add(parts_last.at[d, near[d]], to.at[d])
                self.arrive.append(send(parts_last.at[d, near[d]], ta.at[d, d], ways[d], "ta", d, d))

        def gather(self):
            for c in self.arrive:
                c.wait_recv()

            def total(x):
                return parts_last[x, y].astype(F32) + ta[0, x].astype(F32) + ta[1, x].astype(F32)

            ts[...] = total(xo).astype(BF)
            self.last = send(ts, tx, cross, "tx")
            tacc[...] = total(xm)

        def end(self):
            self.last.wait_recv()
            gate = tacc[...] + tx[...].astype(F32)
            up = pltpu.roll(gate, 64, 1)
            h = gate / (1 + jnp.exp(-gate)) * up
            hid[:, MAIN:FF] = h[:, 0:LAST].astype(BF)

    along = [Along(i, j) for i, j in enumerate(ALONG)]
    crossed = [Cross(i, j) for i, j in enumerate(CROSS)]
    last = Last()
    waited = len(sent)
    compute_last(c_wt)
    last.start()
    for j in range(1, AHEAD):
        merge(j, 0)
    for j in range(CHUNKS):
        compute(j, crossed[CROSS.index(j)] if j in CROSS else along[ALONG.index(j)])
        if j + AHEAD < CHUNKS:
            merge(j + AHEAD, 0)
    along[0].forward()
    along[1].forward()
    crossed[0].turn()
    along[2].forward()
    along[3].forward()
    last.forward()
    along[0].gather()
    crossed[0].forward()
    crossed[1].turn()
    along[1].gather()
    crossed[1].forward()
    along[2].gather()
    crossed[0].end()
    for c in sent[:waited]:
        c.wait_send()
    for j in range(CHUNKS):
        swap(j).wait_send()

    @pl.when(even)
    def _():
        for p in range(PARTS):
            far(p, 0, ys).wait_send()
            for q in range(2):
                for d in range(2):
                    hop(d, 1, q, p, z).wait_send()
                    hop(d, 3, q, p, source(d, 2)).wait_send()

    @pl.when(odd)
    def _():
        for p in range(PARTS):
            t0[p].wait_send()
            far(p, 1, ys).wait_send()
            for q in range(2):
                for d in range(2):
                    hop(d, 2, q, p, source(d, 1)).wait_send()
                    if d == q:
                        hop(d, 4, q, p, source(d, 3)).wait_send()

    crossed[2].turn()
    along[3].gather()
    last.gather()
    crossed[2].forward()
    crossed[1].end()
    along[0].end()
    along[1].end()
    along[2].end()
    along[3].end()
    last.end()
    crossed[2].end()

    for c in sent[waited:]:
        c.wait_send()
    assert len(names.names) <= COPIES, len(names.names)


def store(a, b, c, x, y, z, sems):
    copies = [
        pltpu.make_async_copy(src, dst, sems.at[i]) for i, (src, dst) in enumerate(((a, x), (b, y), (c, z)))
    ]
    for c in copies:
        c.start()
    for c in copies:
        c.wait()


COPIES = 192
PARTS = 2
AHEAD = 2
PART = ROWS // PARTS


def body(tokens, gate_weight, up_weight, gate_lower, up_lower, *others):
    args = (
        tokens, gate_weight.T, up_weight.T, gate_lower.swapaxes(1, 2), up_lower.swapaxes(1, 2), *others
    )
    vmem = pl.BlockSpec(memory_space=pltpu.VMEM)
    smem = pl.BlockSpec(memory_space=pltpu.SMEM)
    anywhere = pl.BlockSpec(memory_space=pl.ANY)
    n_a, n_c = len(ALONG), len(CROSS)

    def b(*shape):
        return pltpu.VMEM(shape, BF)

    def f(*shape):
        return pltpu.VMEM(shape, F32)

    scratch = [
        b(ROWS, DEPTH), b(1, RANK, DEPTH), b(1, RANK, DEPTH), b(1, RANK, FF), b(1, RANK, FF),
        b(2, 4, ROWS, 2 * DEPTH),
        b(FF, DEPTH), b(FF, DEPTH),
        b(CHUNKS, 2, WIDE, 2 * DEPTH),
        b(128, 2 * DEPTH),
        b(16, 16, DEPTH), b(8, 16, DEPTH), b(8, 16, DEPTH), b(7, 16, DEPTH), b(16, 16, DEPTH),
        b(2, 8, 16, FF), b(8, 16, FF), b(8, 16, FF), b(3, 2, 16, FF), b(2, 16, FF), b(16, FF), b(2, 8, 16, FF),
        b(CHUNKS, 2, 2, 4, ROWS, WIDE),
        b(2, 4, ROWS, 128),
        b(n_c, 2, 4, ROWS, WIDE), b(n_c, 2, ROWS, WIDE), b(n_c, 2, 2, ROWS, WIDE),
        b(n_a, 2, 2, ROWS, WIDE), b(n_a, 2, 2, 2, ROWS, WIDE),
        f(n_a, 2, ROWS, WIDE), b(n_a, 2, ROWS, WIDE), b(n_a, 2, ROWS, WIDE),
        b(2, ROWS, 128), b(2, 2, ROWS, 128), f(ROWS, 128), b(ROWS, 128), b(ROWS, 128),
        pltpu.SemaphoreType.DMA((COPIES,)), pltpu.SemaphoreType.DMA((COPIES,)), pltpu.SemaphoreType.DMA((7,)),
    ]
    new_gate, new_up, hidden = pl.pallas_call(
        kernel,
        out_shape=(
            pltpu.VMEM((FF, DEPTH), BF),
            pltpu.VMEM((FF, DEPTH), BF),
            pltpu.VMEM((ROWS, FF), BF),
        ),
        in_specs=[anywhere] * 7 + [smem] * 2,
        out_specs=(vmem, vmem, vmem),
        scratch_shapes=scratch,
        compiler_params=pltpu.CompilerParams(
            collective_id=0, has_side_effects=True, vmem_limit_bytes=56 * 1024 * 1024
        ),
        cost_estimate=pl.CostEstimate(flops=7_000_000_000, bytes_accessed=10_000_000, transcendentals=200_000),
    )(*args)
    new_gate, new_up, hidden = pl.pallas_call(
        store,
        out_shape=(
            jax.ShapeDtypeStruct((FF, DEPTH), BF),
            jax.ShapeDtypeStruct((FF, DEPTH), BF),
            jax.ShapeDtypeStruct((ROWS, FF), BF),
        ),
        in_specs=[anywhere] * 3,
        out_specs=(anywhere,) * 3,
        scratch_shapes=[pltpu.SemaphoreType.DMA((3,))],
        compiler_params=pltpu.CompilerParams(vmem_limit_bytes=1024 * 1024),
    )(new_gate, new_up, hidden)
    return new_gate.T, new_up.T, hidden


def solution(mesh):
    return jax.shard_map(
        body,
        mesh=mesh,
        in_specs=(
            P("col", "row"),
            P("row", "col"),
            P("row", "col"),
            P("col", "row", None),
            P("col", "row", None),
            P("row", None, "col"),
            P("row", None, "col"),
            P(),
            P(),
        ),
        out_specs=(P("row", "col"), P("row", "col"), P("row", "col")),
        check_vma=False,
    )
```
